512 devices in a mesh: pool: 16 (over z), row: 8 (over y, core), head: 4 (over x).
Axes of the slice: x: 4, y: 4, z: 16, core: 2. Of those that a mesh axis runs over, the one named last changes fastest.
Arguments:
- queries: bfloat16 [2048, 64, 128], P(('pool', 'row'), 'head'), may hold values from -24 to 24
- prefix_keys: bfloat16 [16, 8192, 8, 128], P('pool', 'row', 'head'), may hold values from -18 to 18
- prefix_values: bfloat16 [16, 8192, 8, 128], P('pool', 'row', 'head'), may hold values from -6 to 6
- suffix_keys: bfloat16 [2048, 64, 8, 128], P(('pool', 'row'), None, 'head'), may hold values from -18 to 18
- suffix_values: bfloat16 [2048, 64, 8, 128], P(('pool', 'row'), None, 'head'), may hold values from -6 to 6
- row_prefix: int32 [2048, 1], P(('pool', 'row')), may hold values from 0 to 15; in each aligned block of 16 rows (0 to 15, 16 to 31, ...) at most 3 rows name the same one
- owner_map: int32 [16], replicated, may hold values from 0 to 15, each once
- prefix_lengths: int32 [16], replicated, may hold values from 2048 to 8192, as said below
- suffix_lengths: int32 [2048], P(('pool', 'row')), may hold values from 1 to 64, as said below
- out_weight: bfloat16 [8192, 5120], P('head', 'row'), may hold values from -2 to 2
Outputs:
- projected: bfloat16 [2048, 5120], P(('pool', 'head'), 'row')
The draws below stay inside these ranges and needn't reach their ends.
Inputs may be any that keep to these rules, and one draw needn't show every extreme that they name: `row_prefix`: among the rows of one index of pool and row, no prefix id is named more than 3 times, a bound that some block reaches. `owner_map`: each index of pool owns exactly one prefix id. `prefix_lengths`: every prefix holds at least a quarter of 8192 positions; the longest holds exactly 8192. `suffix_lengths`: some row has exactly 64 suffix positions.
All inputs are finite; a program needn't handle non-finite values.
Results may differ from the reference program's by a relative error of at most 0.019.
Values may be sent and summed in bfloat16 or wider, within the bound.
No kernel may reach another device: no remote copies, remote signals or barrier semaphores. Data moves between devices by JAX's collectives and lax.ppermute only.
A program may use at most 128 MiB of HBM per device.

```python
import math
import jax
import jax.numpy as jnp
import numpy as np
from jax import lax

QH = 64
KVH = 8
HD = 128
D = 5120
ROWS_DEV = 16
PLEN_DEV = 1024
SUF = 64
ROWS = 2048
NPREF = 16
PLEN = 8192
CAP = 3


def drawn_draw(key, shape):
    own_key = jax.random.fold_in(key, shape[0] * 7 + shape[1] * 3 + 11)
    base = jax.random.truncated_normal(own_key, -6.0, 6.0, shape, jnp.float32)
    return base


def draw_queries(key, part):
    return drawn_draw(key, (ROWS, QH, HD)).astype(jnp.bfloat16)


def draw_prefix_keys(key, part):
    return drawn_draw(key, (NPREF, PLEN, KVH, HD)).astype(jnp.bfloat16)


def draw_suffix_keys(key, part):
    return drawn_draw(key, (ROWS, SUF, KVH, HD)).astype(jnp.bfloat16)


def draw_prefix_lengths(key, part):
    key = jax.random.fold_in(key, 5)
    lengths = jax.random.randint(key, (NPREF,), PLEN // 4, PLEN + 1, jnp.int32)
    longest = jax.random.randint(jax.random.fold_in(key, 1), (), 0, NPREF, jnp.int32)
    return jnp.where(jnp.arange(NPREF, dtype=jnp.int32) == longest, PLEN, lengths).astype(jnp.int32)


def draw_suffix_lengths(key, part):
    key = jax.random.fold_in(key, 6)
    lengths = jax.random.randint(key, (ROWS,), 1, SUF + 1, jnp.int32)
    longest = jax.random.randint(jax.random.fold_in(key, 1), (), 0, ROWS, jnp.int32)
    return jnp.where(jnp.arange(ROWS, dtype=jnp.int32) == longest, SUF, lengths).astype(jnp.int32)


def block_scale(rng, dims, cuts, low, top_value):
    level = 1.0
    for position, parts in cuts:
        draws = jax.random.uniform(jax.random.fold_in(jax.random.fold_in(rng, 6), position), (parts,), jnp.float32, low / len(cuts), top_value / len(cuts))
        level = level * jnp.repeat(jnp.exp(draws), dims[position] // parts).reshape((-1,) + (1,) * (len(dims) - 1 - position))
    return level


def deal_out(key, own, number, rows, count, top, limit, skew):
    order = jax.random.permutation(key, count)
    heavy_load, ordinary = shares(count, rows * top, limit, skew, True), shares(count, rows * top, limit, skew, False)
    places = jnp.arange(count)

    def named(sizes, rotation):
        used = int((sizes > 0).sum())
        fixed = max(1, used // 4)
        moved = fixed + (places - fixed + rotation * (used - fixed)) % max(1, count - fixed)
        return jnp.zeros((count,), jnp.int32).at[order[jnp.where(places < fixed, places, moved)]].set(jnp.asarray(sizes, jnp.int32))

    sizes = jnp.where(number % 4 == 0, named(heavy_load, number // 4), named(ordinary, number - number // 4 - 1))
    mixed = jax.random.permutation(jax.random.fold_in(own, 3), count)
    donor, taker = mixed[0:count // 2 * 2:2], mixed[1:count // 2 * 2:2]
    room = jnp.minimum(sizes[donor] - 1, limit - sizes[taker]) // 2
    room = jnp.where((donor == order[0]) | (taker == order[0]) | (sizes[taker] == 0), 0, jnp.maximum(room, 0))
    moved = jax.random.randint(jax.random.fold_in(own, 4), (count // 2,), 0, 1 << 20) % (room + 1)
    sizes = sizes.at[donor].add(-moved).at[taker].add(moved)
    items = jnp.searchsorted(jnp.cumsum(sizes), jnp.arange(rows * top), side="right").astype(jnp.int32)
    listing = items.reshape(top, rows).T
    listing = listing[jax.random.permutation(jax.random.fold_in(own, 1), rows)]
    rotation = jax.random.randint(jax.random.fold_in(own, 2), (rows, 1), 0, top)
    return jnp.take_along_axis(listing, (jnp.arange(top)[None, :] + rotation) % top, axis=1)


def shares(amount, total, limit, slope, full):
    portions = [(1 << 20) // math.isqrt(rank ** slope) + 1 for rank in range(1, amount + 1)]
    largest = limit if full else min(limit, max(-(-total // amount), total * portions[0] // sum(portions)))
    least = 1 if total - largest >= amount - 1 else 0
    given, rest = [largest] + [least] * (amount - 1), total - largest - least * (amount - 1)
    while rest > 0:
        free = [i for i in range(1, amount) if given[i] < largest] or [i for i in range(1, amount) if given[i] < limit]
        pool, budget = sum([portions[i] for i in free]), rest
        for i in free:
            addition = min(limit - given[i], max(1, budget * portions[i] // pool), rest)
            given[i] = given[i] + addition
            rest = rest - addition
    return np.array(given)


def gaussian(key, dims, scale, reach, split=(), held_as=jnp.bfloat16):
    drawn = jax.random.normal(key, dims, jnp.float32) * scale
    if len(split) > 0:
        drawn = block_scale(key, dims, split, -0.22, 0.18) * drawn
    return jnp.clip(drawn, min=-reach, max=reach).astype(held_as)


def setup_inputs(seed: int = 0) -> dict:
    streams_of = jax.random.split(jax.random.key(seed), 11)
    queries = draw_queries(jax.random.fold_in(streams_of[10], 71), 0)
    prefix_keys = draw_prefix_keys(jax.random.fold_in(streams_of[10], 71), 0)
    prefix_values = gaussian(streams_of[2], (NPREF, PLEN, KVH, HD), 1.0, 6.0, ((0, 16), (1, 8), (2, 4)))
    suffix_keys = draw_suffix_keys(jax.random.fold_in(streams_of[10], 71), 0)
    suffix_values = gaussian(streams_of[4], (ROWS, SUF, KVH, HD), 1.0, 6.0, ((0, 128), (2, 4)))
    row_prefix_keys = jax.random.split(jax.random.fold_in(streams_of[5], 1), ROWS // ROWS_DEV)
    row_prefix_turns = jax.random.permutation(jax.random.fold_in(streams_of[5], 3), ROWS // ROWS_DEV)
    row_prefix = jax.vmap(lambda own, number: deal_out(jax.random.fold_in(streams_of[5], 2), own, number, ROWS_DEV, NPREF, 1, CAP, 2))(row_prefix_keys, row_prefix_turns).reshape((ROWS, 1))
    owner_map = jax.random.permutation(streams_of[6], NPREF).astype(jnp.int32)
    prefix_lengths = draw_prefix_lengths(jax.random.fold_in(streams_of[10], 71), 0)
    suffix_lengths = draw_suffix_lengths(jax.random.fold_in(streams_of[10], 71), 0)
    out_weight = gaussian(streams_of[9], (QH * HD, D), (max(1, QH * HD // 1024)) ** -0.5, 2.0, ((0, 4), (1, 8)))
    return dict(queries=queries, prefix_keys=prefix_keys, prefix_values=prefix_values, suffix_keys=suffix_keys, suffix_values=suffix_values, row_prefix=row_prefix, owner_map=owner_map, prefix_lengths=prefix_lengths, suffix_lengths=suffix_lengths, out_weight=out_weight)


LOWEST = -1.0e30


def softmax_parts(grouped, key_rows, value_rows, length):
    scores = jnp.einsum("kgd,tkd->kgt", grouped, key_rows.astype(jnp.float32)) * (HD ** -0.5)
    visible = jnp.arange(key_rows.shape[0], dtype=jnp.int32) < length
    masked = jnp.where(visible, scores, -jnp.inf)
    peak = jnp.max(masked, axis=-1)
    peak = jnp.where(jnp.isfinite(peak), peak, jnp.zeros_like(peak))
    powers = jnp.where(visible, jnp.exp(scores - peak[..., None]), jnp.zeros_like(scores))
    total = jnp.sum(powers, axis=-1)
    weights = lax.optimization_barrier(powers.astype(jnp.bfloat16))
    weighted = jnp.einsum("kgt,tkd->kgd", weights.astype(jnp.float32), value_rows.astype(jnp.float32))
    live = total > 0
    safe_total = jnp.where(live, total, jnp.ones_like(total))
    block_out = jnp.where(live[..., None], weighted / safe_total[..., None], jnp.zeros_like(weighted))
    block_lse = jnp.where(live, peak + jnp.log(safe_total), jnp.full_like(total, LOWEST))
    return block_out, block_lse


def reference(queries, prefix_keys, prefix_values, suffix_keys, suffix_values, row_prefix, owner_map, prefix_lengths, suffix_lengths, out_weight):
    blocks = PLEN // PLEN_DEV

    def one_row(items):
        query_row, prefix_id, suffix_length, suffix_key, suffix_value = items
        owner = owner_map[prefix_id]
        key_rows = lax.dynamic_index_in_dim(prefix_keys, owner, 0, keepdims=False).reshape(blocks, PLEN_DEV, KVH, HD)
        value_rows = lax.dynamic_index_in_dim(prefix_values, owner, 0, keepdims=False).reshape(blocks, PLEN_DEV, KVH, HD)
        grouped = query_row.astype(jnp.float32).reshape(KVH, QH // KVH, HD)
        starts = jnp.arange(blocks, dtype=jnp.int32) * PLEN_DEV
        block_lengths = jnp.clip(prefix_lengths[prefix_id] - starts, 0, PLEN_DEV).astype(jnp.int32)
        block_out, block_lse = jax.vmap(lambda k, v, n: softmax_parts(grouped, k, v, n))(key_rows, value_rows, block_lengths)
        block_out = lax.optimization_barrier(block_out.astype(jnp.bfloat16)).astype(jnp.float32)
        top = jnp.max(block_lse, axis=0)
        share = jnp.exp(block_lse - top)
        share_total = jnp.sum(share, axis=0)
        prefix_out = jnp.sum(share[..., None] * block_out, axis=0) / share_total[..., None]
        prefix_lse = top + jnp.log(share_total)
        suffix_out, suffix_lse = softmax_parts(grouped, suffix_key, suffix_value, suffix_length)
        highest = jnp.maximum(prefix_lse, suffix_lse)
        prefix_share = jnp.exp(prefix_lse - highest)
        suffix_share = jnp.exp(suffix_lse - highest)
        mixed = (prefix_share[..., None] * prefix_out + suffix_share[..., None] * suffix_out) / (prefix_share + suffix_share)[..., None]
        return mixed.reshape(QH * HD).astype(jnp.bfloat16)

    attended = lax.map(one_row, (queries, row_prefix[:, 0], suffix_lengths, suffix_keys, suffix_values))
    projected = jnp.dot(attended, out_weight, preferred_element_type=jnp.float32).astype(jnp.bfloat16)
    return projected
```

```python
import functools
import math

import jax
import jax.numpy as jnp
from jax import lax
from jax.experimental import pallas as pl
from jax.experimental.pallas import tpu as pltpu
from jax.sharding import Mesh, PartitionSpec as P

LOWEST = -1e30
CAP = 3
GROUP = 8
HD = 128
SCALE = HD**-0.5
LOG2E = math.log2(math.e)
F32 = jnp.float32
BF16 = jnp.bfloat16

VMEM = pl.BlockSpec(memory_space=pltpu.VMEM)
SMEM = pl.BlockSpec(memory_space=pltpu.SMEM)


def params(mib):
    return pltpu.CompilerParams(vmem_limit_bytes=mib * 1024 * 1024)


def split3(value):
    high = value.astype(BF16).astype(F32)
    rest = value - high
    middle = rest.astype(BF16).astype(F32)
    return high, middle, (rest - middle).astype(BF16).astype(F32)


def slot_of(row, row_prefix_ref, owner_ref, count_ref):
    owner = owner_ref[row_prefix_ref[row]]
    place = count_ref[owner]
    count_ref[owner] = place + 1
    return owner, place


def dispatch_kernel(row_prefix_ref, owner_ref, q_ref, out_ref, count_ref):
    for p in range(owner_ref.shape[0]):
        count_ref[p] = 0
    out_ref[...] = jnp.zeros_like(out_ref)
    for r in range(q_ref.shape[0]):
        owner, place = slot_of(r, row_prefix_ref, owner_ref, count_ref)
        out_ref[owner * CAP + place] = q_ref[r]


def unmix_kernel(k0_ref, k1_ref, v0_ref, v1_ref, k_ref, v_ref, scratch):
    length = k0_ref.shape[0] // 2
    for i, (sources, target) in enumerate((((k0_ref, k1_ref), k_ref), ((v0_ref, v1_ref), v_ref))):
        for n, source in enumerate(sources):
            held = scratch.at[2 * i + n]
            held[...] = source[...].astype(F32)
            for g in range(2):
                target[g, n * length : (n + 1) * length, :] = held[
                    pl.ds(g, length, stride=2), :
                ].astype(BF16)


def attend_kernel(owner_ref, lengths_ref, q_ref, k_ref, v_ref, out_ref):
    slots = q_ref.shape[0]
    step_slots = math.gcd(24, slots)
    span = k_ref.shape[1]
    part = span // 2
    pool = lax.axis_index("pool")
    core = lax.axis_index("core")
    first = lax.axis_index("y") * 2
    own_length = jnp.int32(0)
    for p in range(owner_ref.shape[0]):
        own_length += jnp.where(owner_ref[p] == pool, lengths_ref[p], 0)
    column = lax.broadcasted_iota(jnp.int32, (1, span), 1)
    token = jnp.where(
        column < part, column + (first + core) * part, column + (first - core) * part
    )
    bias = jnp.where(token < own_length, 0.0, LOWEST).astype(F32)
    lane = lax.broadcasted_iota(jnp.int32, (GROUP, 128), 1)

    def step(j, packed):
        start = j * step_slots
        q_all = q_ref[pl.ds(start, step_slots)].astype(F32)
        outs = []
        filled = []
        for g in range(2):
            q = q_all[:, g * GROUP : (g + 1) * GROUP, :].reshape(step_slots * GROUP, HD)
            scores = (
                lax.dot_general(
                    q.astype(BF16), k_ref[g], (((1,), (1,)), ((), ())), preferred_element_type=F32
                )
                + bias
            )
            peak = jnp.maximum(jnp.max(scores, axis=1, keepdims=True), 0.1 * LOWEST)
            weights = jnp.exp2((scores - peak) * (SCALE * LOG2E)).astype(BF16)
            values = jnp.concatenate([v_ref[g], jnp.ones((span, HD), BF16)], axis=1)
            both = jnp.dot(weights, values, preferred_element_type=F32)
            total = both[:, HD:]
            live = total > 0
            safe = jnp.where(live, total, 1.0)
            outs.append((both[:, :HD] / safe).reshape(step_slots, GROUP, HD))
            lse = jnp.where(live, peak * SCALE + jnp.log(safe), LOWEST)
            lse = lse.reshape(step_slots, GROUP, HD)
            kept = packed[g]
            for i in range(step_slots):
                kept = jnp.where(lane == start + i, lse[i], kept)
            filled.append(kept)
        out_ref[pl.ds(start, step_slots)] = jnp.concatenate(outs, axis=1).astype(BF16)
        return tuple(filled)

    empty = jnp.zeros((GROUP, 128), F32)
    packed = lax.fori_loop(0, slots // step_slots, step, (empty, empty))
    for i, plane in enumerate(split3(jnp.concatenate(packed, axis=0))):
        out_ref[slots + i] = plane.astype(BF16)


def merge_kernel(a_ref, b_ref, c_ref, d_ref, out_ref):
    blocks = (a_ref, b_ref, c_ref, d_ref)
    slots = a_ref.shape[0] - 3
    pools = slots // CAP
    lses = [
        (ref[slots + 2].astype(F32) + ref[slots + 1].astype(F32)) + ref[slots].astype(F32)
        for ref in blocks
    ]
    top = functools.reduce(jnp.maximum, lses)
    shares = [jnp.exp(lse - top) for lse in lses]
    total = functools.reduce(jnp.add, shares)
    weights = [share / total for share in shares]
    planes = split3(top + jnp.log(total))
    lane = lax.broadcasted_iota(jnp.int32, (GROUP, 128), 1)
    for pair in range(0, pools, 2):
        rows = []
        for p in (pair, pair + 1):
            for s in range(p * CAP, (p + 1) * CAP):
                terms = [
                    weight[:, s : s + 1] * ref[s].astype(F32) for weight, ref in zip(weights, blocks)
                ]
                rows.append(functools.reduce(jnp.add, terms))
            tile = jnp.zeros((GROUP, 128), F32)
            for i, plane in enumerate(planes):
                for g in range(2):
                    at = i * 16 + g * 8
                    moved = plane[g * GROUP : (g + 1) * GROUP]
                    shift = (at - p * CAP) % 128
                    if shift:
                        moved = pltpu.roll(moved, shift, 1)
                    tile = jnp.where((lane >= at) & (lane < at + CAP), moved, tile)
            rows.append(tile)
        height = CAP * 16 + GROUP
        out_ref[pl.ds(pair * height, 2 * height), :] = jnp.concatenate(rows, axis=0).astype(BF16)


def suffix_kernel(length_ref, q_ref, k_ref, v_ref, out_ref, lse_ref):
    span = k_ref.shape[1]
    column = lax.broadcasted_iota(jnp.int32, (2 * GROUP, span), 1)
    head = lax.broadcasted_iota(jnp.int32, (2 * GROUP, span), 0)
    same = (column & 1) == head // GROUP
    for r in range(q_ref.shape[0]):
        scores = lax.dot_general(
            q_ref[r], k_ref[r], (((1,), (1,)), ((), ())), preferred_element_type=F32
        )
        visible = same & (column < 2 * length_ref[r])
        scores = jnp.where(visible, scores * SCALE, LOWEST)
        peak = jnp.max(scores, axis=1, keepdims=True)
        powers = jnp.exp(scores - peak)
        total = jnp.sum(powers, axis=1, keepdims=True)
        summed = jnp.dot(powers.astype(BF16), v_ref[r], preferred_element_type=F32)
        out_ref[r] = summed / total
        lse_ref[r] = jnp.broadcast_to(peak + jnp.log(total), (2 * GROUP, HD))


def combine_kernel(
    row_prefix_ref, owner_ref, got_ref, suffix_ref, suffix_lse_ref, out_ref, wide, mixed, count_ref
):
    rows = suffix_ref.shape[0]
    height = CAP * 16 + GROUP
    for p in range(owner_ref.shape[0]):
        count_ref[p] = 0
    wide[...] = got_ref[...].astype(F32)
    lane = lax.broadcasted_iota(jnp.int32, (GROUP, 128), 1)
    for r in range(rows):
        owner, place = slot_of(r, row_prefix_ref, owner_ref, count_ref)
        base = owner * height
        prefix = wide[pl.ds(pl.multiple_of(base + place * 16, 8), 16), :]
        tile = wide[pl.ds(pl.multiple_of(base + CAP * 16, 8), GROUP), :]
        lses = []
        for g in range(2):
            chosen = ((lane & 15) == place + g * 8) & (lane < 48)
            lses.append(jnp.sum(jnp.where(chosen, tile, 0.0), axis=1, keepdims=True))
        prefix_lse = jnp.broadcast_to(jnp.concatenate(lses, axis=0), (2 * GROUP, HD))
        suffix_lse = suffix_lse_ref[r]
        highest = jnp.maximum(prefix_lse, suffix_lse)
        a = jnp.exp(prefix_lse - highest)
        b = jnp.exp(suffix_lse - highest)
        mixed[r * 16 : (r + 1) * 16, :] = (a * prefix + b * suffix_ref[r]) / (a + b)
    for h in range(2 * GROUP):
        piece = mixed[pl.ds(h, rows, stride=16), :].astype(BF16)
        for n in range(out_ref.shape[0]):
            out_ref[n, :, h * HD : (h + 1) * HD] = piece


def project_kernel(own_ref, other_ref, w_ref, out_ref):
    count, rows, depth = own_ref.shape
    core = lax.axis_index("core")
    both = jnp.concatenate(
        [own_ref[...].reshape(count * rows, depth), other_ref[...].reshape(count * rows, depth)],
        axis=0,
    )
    terms = jnp.dot(both, w_ref[...], preferred_element_type=F32).astype(BF16)
    terms = terms.reshape(2, count, rows, -1)
    for n in range(count):
        out_ref[n, core] = terms[0, n]
        out_ref[n, 1 - core] = terms[1, n]


def body(
    queries,
    prefix_keys,
    prefix_values,
    suffix_keys,
    suffix_values,
    row_prefix,
    owner_map,
    prefix_lengths,
    suffix_lengths,
    out_weight,
):
    rows, heads, hdim = queries.shape
    row_prefix = row_prefix.reshape(-1)
    pools = lax.axis_size("pool")
    ring = lax.axis_size("y")
    slots = pools * CAP
    columns = out_weight.shape[1]
    shape = jax.ShapeDtypeStruct

    def turn(value, by):
        return lax.ppermute(value, "y", [(i, (i + by) % ring) for i in range(ring)])

    def swap(value):
        return lax.ppermute(value, "core", [(0, 1), (1, 0)])

    outgoing = pl.pallas_call(
        dispatch_kernel,
        out_shape=shape((slots, heads, hdim), BF16),
        in_specs=[SMEM, SMEM, VMEM],
        out_specs=VMEM,
        scratch_shapes=[pltpu.SMEM((pools,), jnp.int32)],
        compiler_params=params(8),
        cost_estimate=pl.CostEstimate(flops=0, bytes_accessed=300_000, transcendentals=0),
        name="dispatch",
    )(row_prefix, owner_map, queries)

    own_keys = prefix_keys.reshape(-1, hdim)
    own_values = prefix_values.reshape(-1, hdim)
    other_keys = swap(prefix_keys).reshape(-1, hdim)
    other_values = swap(prefix_values).reshape(-1, hdim)

    arrived = lax.all_to_all(
        outgoing.reshape(pools, CAP, heads, hdim), "pool", split_axis=0, concat_axis=0, tiled=True
    ).reshape(slots, heads, hdim)
    asked = {by: turn(arrived, by) for by in (1, ring - 1, 2)}
    asked[0] = arrived

    span = own_keys.shape[0]
    keys, values = pl.pallas_call(
        unmix_kernel,
        out_shape=[shape((2, span, hdim), BF16)] * 2,
        in_specs=[VMEM] * 4,
        out_specs=[VMEM] * 2,
        scratch_shapes=[pltpu.VMEM((4, span, hdim), F32)],
        compiler_params=params(16),
        cost_estimate=pl.CostEstimate(flops=0, bytes_accessed=4_000_000, transcendentals=0),
        name="unmix",
    )(own_keys, other_keys, own_values, other_values)

    suffix_out, suffix_lse = pl.pallas_call(
        suffix_kernel,
        out_shape=[shape((rows, heads, hdim), F32)] * 2,
        in_specs=[SMEM, VMEM, VMEM, VMEM],
        out_specs=[VMEM] * 2,
        compiler_params=params(8),
        cost_estimate=pl.CostEstimate(
            flops=4 * rows * heads * 128 * 128, bytes_accessed=2_000_000, transcendentals=0
        ),
        name="suffix",
    )(
        suffix_lengths,
        queries,
        suffix_keys.reshape(rows, -1, hdim),
        suffix_values.reshape(rows, -1, hdim),
    )

    attend = pl.pallas_call(
        attend_kernel,
        out_shape=shape((slots + 3, heads, hdim), BF16),
        in_specs=[SMEM, SMEM, VMEM, VMEM, VMEM],
        out_specs=VMEM,
        compiler_params=params(24),
        cost_estimate=pl.CostEstimate(
            flops=6 * slots * heads * span * hdim,
            bytes_accessed=3_000_000,
            transcendentals=slots * heads * span,
        ),
        name="attend",
    )
    parts = {by: attend(owner_map, prefix_lengths, q, keys, values) for by, q in asked.items()}
    merged = pl.pallas_call(
        merge_kernel,
        out_shape=shape((pools * (CAP * heads + GROUP), hdim), BF16),
        in_specs=[VMEM] * 4,
        out_specs=VMEM,
        compiler_params=params(8),
        cost_estimate=pl.CostEstimate(flops=0, bytes_accessed=1_000_000, transcendentals=0),
        name="merge",
    )(parts[0], *(turn(parts[by], -by) for by in (1, ring - 1, 2)))
    returned = lax.all_to_all(
        merged.reshape(pools, CAP * heads + GROUP, hdim),
        "pool",
        split_axis=0,
        concat_axis=0,
        tiled=True,
    ).reshape(-1, hdim)

    attended = pl.pallas_call(
        combine_kernel,
        out_shape=shape((ring, rows, heads * hdim), BF16),
        in_specs=[SMEM, SMEM, VMEM, VMEM, VMEM],
        out_specs=VMEM,
        scratch_shapes=[
            pltpu.VMEM((pools * (CAP * heads + GROUP), hdim), F32),
            pltpu.VMEM((rows * heads, hdim), F32),
            pltpu.SMEM((pools,), jnp.int32),
        ],
        compiler_params=params(8),
        cost_estimate=pl.CostEstimate(flops=0, bytes_accessed=1_000_000, transcendentals=0),
        name="combine",
    )(row_prefix, owner_map, returned, suffix_out, suffix_lse)
    gathered = lax.all_to_all(attended, "y", split_axis=0, concat_axis=0, tiled=True)
    terms = pl.pallas_call(
        project_kernel,
        out_shape=shape((ring, 2, rows, columns), BF16),
        in_specs=[VMEM] * 3,
        out_specs=VMEM,
        compiler_params=params(16),
        cost_estimate=pl.CostEstimate(
            flops=4 * ring * rows * heads * hdim * columns,
            bytes_accessed=4_000_000,
            transcendentals=0,
        ),
        name="project",
    )(gathered, swap(gathered), out_weight)
    shared = lax.all_to_all(
        terms.reshape(lax.axis_size("head"), -1, columns), "head", split_axis=0, concat_axis=0, tiled=True
    )
    return jnp.sum(shared.astype(F32), axis=0).astype(BF16)


def solution(mesh):
    pools, across, groups = mesh.devices.shape
    fine = Mesh(
        mesh.devices.reshape(pools, across // 2, 2, groups), ("pool", "y", "core", "head")
    )
    row = ("y", "core")
    every = ("pool", "y", "core")
    return jax.shard_map(
        body,
        mesh=fine,
        in_specs=(
            P(every, "head", None),
            P("pool", row, "head", None),
            P("pool", row, "head", None),
            P(every, None, "head", None),
            P(every, None, "head", None),
            P(every, None),
            P(),
            P(),
            P(every),
            P("head", row),
        ),
        out_specs=P(("pool", "head"), row),
        check_vma=False,
    )
```

```python
import functools
import math

import jax
import jax.numpy as jnp
from jax import lax
from jax.experimental import pallas as pl
from jax.experimental.pallas import tpu as pltpu
from jax.sharding import Mesh, PartitionSpec as P

LOWEST = -1e30
CAP = 3
GROUP = 8
HD = 128
SCALE = HD**-0.5
LOG2E = math.log2(math.e)
F32 = jnp.float32
BF16 = jnp.bfloat16

VMEM = pl.BlockSpec(memory_space=pltpu.VMEM)
SMEM = pl.BlockSpec(memory_space=pltpu.SMEM)


def params(mib):
    return pltpu.CompilerParams(vmem_limit_bytes=mib * 1024 * 1024)


def split3(value):
    high = value.astype(BF16).astype(F32)
    rest = value - high
    middle = rest.astype(BF16).astype(F32)
    return high, middle, (rest - middle).astype(BF16).astype(F32)


def slot_of(row, row_prefix_ref, owner_ref, count_ref):
    owner = owner_ref[row_prefix_ref[row]]
    place = count_ref[owner]
    count_ref[owner] = place + 1
    return owner, place


def dispatch_kernel(
    row_prefix_ref, owner_ref, q_ref, k_ref, v_ref, out_ref, packed_ref, held, count_ref
):
    for p in range(owner_ref.shape[0]):
        count_ref[p] = 0
    out_ref[...] = jnp.zeros_like(out_ref)
    for r in range(q_ref.shape[0]):
        owner, place = slot_of(r, row_prefix_ref, owner_ref, count_ref)
        out_ref[owner * CAP + place] = q_ref[r]
    length = packed_ref.shape[1]
    for n, source in enumerate((k_ref, v_ref)):
        held[n] = source[...].astype(F32)
        for g in range(2):
            packed_ref[2 * n + g] = held[n, pl.ds(g, length, stride=2), :].astype(BF16)


def attend_kernel(sources, owner_ref, lengths_ref, q_ref, *refs):
    blocks, out_ref = refs[:-1], refs[-1]
    slots = q_ref.shape[0]
    step_slots = math.gcd(24, slots)
    span = blocks[0].shape[1]
    pool = lax.axis_index("pool")
    core = lax.axis_index("core")
    across = lax.axis_index("y")
    own_length = jnp.int32(0)
    for p in range(owner_ref.shape[0]):
        own_length += jnp.where(owner_ref[p] == pool, lengths_ref[p], 0)
    column = lax.broadcasted_iota(jnp.int32, (1, span), 1)
    biases = []
    for dy, dc in sources:
        at = (across + dy * (1 - 2 * (across & 1))) * 2 + core + dc * (1 - 2 * core)
        biases.append(jnp.where(column + at * span < own_length, 0.0, LOWEST).astype(F32))
    ones = jnp.ones((span, HD), BF16)
    lane = lax.broadcasted_iota(jnp.int32, (GROUP, 128), 1)

    def step(j, packed):
        start = j * step_slots
        q_all = q_ref[pl.ds(start, step_slots)].astype(F32)
        outs = []
        filled = []
        for g in range(2):
            q = q_all[:, g * GROUP : (g + 1) * GROUP, :].reshape(step_slots * GROUP, HD)
            q = q.astype(BF16)
            scores = [
                lax.dot_general(
                    q, block[g], (((1,), (1,)), ((), ())), preferred_element_type=F32
                )
                + bias
                for block, bias in zip(blocks, biases)
            ]
            peak = functools.reduce(
                jnp.maximum, [jnp.max(part, axis=1, keepdims=True) for part in scores]
            )
            peak = jnp.maximum(peak, 0.1 * LOWEST)
            both = functools.reduce(
                jnp.add,
                [
                    jnp.dot(
                        jnp.exp2((part - peak) * (SCALE * LOG2E)).astype(BF16),
                        jnp.concatenate([block[2 + g], ones], axis=1),
                        preferred_element_type=F32,
                    )
                    for part, block in zip(scores, blocks)
                ],
            )
            total = both[:, HD:]
            live = total > 0
            safe = jnp.where(live, total, 1.0)
            outs.append((both[:, :HD] / safe).reshape(step_slots, GROUP, HD))
            lse = jnp.where(live, peak * SCALE + jnp.log(safe), LOWEST)
            lse = lse.reshape(step_slots, GROUP, HD)
            kept = packed[g]
            for i in range(step_slots):
                kept = jnp.where(lane == start + i, lse[i], kept)
            filled.append(kept)
        out_ref[pl.ds(start, step_slots)] = jnp.concatenate(outs, axis=1).astype(BF16)
        return tuple(filled)

    empty = jnp.zeros((GROUP, 128), F32)
    packed = lax.fori_loop(0, slots // step_slots, step, (empty, empty))
    for i, plane in enumerate(split3(jnp.concatenate(packed, axis=0))):
        out_ref[slots + i] = plane.astype(BF16)


def merge_kernel(a_ref, b_ref, c_ref, out_ref):
    blocks = (a_ref, b_ref, c_ref)
    slots = a_ref.shape[0] - 3
    pools = slots // CAP
    lses = [
        (ref[slots + 2].astype(F32) + ref[slots + 1].astype(F32)) + ref[slots].astype(F32)
        for ref in blocks
    ]
    top = functools.reduce(jnp.maximum, lses)
    shares = [jnp.exp(lse - top) for lse in lses]
    total = functools.reduce(jnp.add, shares)
    weights = [share / total for share in shares]
    planes = split3(top + jnp.log(total))
    lane = lax.broadcasted_iota(jnp.int32, (GROUP, 128), 1)
    for pair in range(0, pools, 2):
        rows = []
        for p in (pair, pair + 1):
            for s in range(p * CAP, (p + 1) * CAP):
                terms = [
                    weight[:, s : s + 1] * ref[s].astype(F32) for weight, ref in zip(weights, blocks)
                ]
                rows.append(functools.reduce(jnp.add, terms))
            tile = jnp.zeros((GROUP, 128), F32)
            for i, plane in enumerate(planes):
                for g in range(2):
                    at = i * 16 + g * 8
                    moved = plane[g * GROUP : (g + 1) * GROUP]
                    shift = (at - p * CAP) % 128
                    if shift:
                        moved = pltpu.roll(moved, shift, 1)
                    tile = jnp.where((lane >= at) & (lane < at + CAP), moved, tile)
            rows.append(tile)
        height = CAP * 16 + GROUP
        out_ref[pl.ds(pair * height, 2 * height), :] = jnp.concatenate(rows, axis=0).astype(BF16)


def suffix_kernel(length_ref, q_ref, k_ref, v_ref, out_ref, lse_ref):
    span = k_ref.shape[1]
    column = lax.broadcasted_iota(jnp.int32, (2 * GROUP, span), 1)
    head = lax.broadcasted_iota(jnp.int32, (2 * GROUP, span), 0)
    same = (column & 1) == head // GROUP
    for r in range(q_ref.shape[0]):
        scores = lax.dot_general(
            q_ref[r], k_ref[r], (((1,), (1,)), ((), ())), preferred_element_type=F32
        )
        visible = same & (column < 2 * length_ref[r])
        scores = jnp.where(visible, scores * SCALE, LOWEST)
        peak = jnp.max(scores, axis=1, keepdims=True)
        powers = jnp.exp(scores - peak)
        total = jnp.sum(powers, axis=1, keepdims=True)
        summed = jnp.dot(powers.astype(BF16), v_ref[r], preferred_element_type=F32)
        out_ref[r] = summed / total
        lse_ref[r] = jnp.broadcast_to(peak + jnp.log(total), (2 * GROUP, HD))


def combine_kernel(
    row_prefix_ref, owner_ref, got_ref, suffix_ref, suffix_lse_ref, out_ref, wide, mixed, count_ref
):
    rows = suffix_ref.shape[0]
    height = CAP * 16 + GROUP
    for p in range(owner_ref.shape[0]):
        count_ref[p] = 0
    wide[...] = got_ref[...].astype(F32)
    lane = lax.broadcasted_iota(jnp.int32, (GROUP, 128), 1)
    for r in range(rows):
        owner, place = slot_of(r, row_prefix_ref, owner_ref, count_ref)
        base = owner * height
        prefix = wide[pl.ds(pl.multiple_of(base + place * 16, 8), 16), :]
        tile = wide[pl.ds(pl.multiple_of(base + CAP * 16, 8), GROUP), :]
        lses = []
        for g in range(2):
            chosen = ((lane & 15) == place + g * 8) & (lane < 48)
            lses.append(jnp.sum(jnp.where(chosen, tile, 0.0), axis=1, keepdims=True))
        prefix_lse = jnp.broadcast_to(jnp.concatenate(lses, axis=0), (2 * GROUP, HD))
        suffix_lse = suffix_lse_ref[r]
        highest = jnp.maximum(prefix_lse, suffix_lse)
        a = jnp.exp(prefix_lse - highest)
        b = jnp.exp(suffix_lse - highest)
        mixed[r * 16 : (r + 1) * 16, :] = (a * prefix + b * suffix_ref[r]) / (a + b)
    for h in range(2 * GROUP):
        piece = mixed[pl.ds(h, rows, stride=16), :].astype(BF16)
        for n in range(out_ref.shape[0]):
            out_ref[n, :, h * HD : (h + 1) * HD] = piece


def project_kernel(attended_ref, w_ref, out_ref):
    out_ref[...] = jnp.dot(
        attended_ref[...], w_ref[...], preferred_element_type=F32
    ).astype(BF16)


def body(
    queries,
    prefix_keys,
    prefix_values,
    suffix_keys,
    suffix_values,
    row_prefix,
    owner_map,
    prefix_lengths,
    suffix_lengths,
    out_weight,
):
    rows, heads, hdim = queries.shape
    row_prefix = row_prefix.reshape(-1)
    pools = lax.axis_size("pool")
    ring = lax.axis_size("y")
    slots = pools * CAP
    columns = out_weight.shape[1]
    shape = jax.ShapeDtypeStruct

    def meet(value, axis, partner):
        return lax.ppermute(value, axis, list(enumerate(partner)))

    length = prefix_keys.shape[1]
    outgoing, own = pl.pallas_call(
        dispatch_kernel,
        out_shape=[shape((slots, heads, hdim), BF16), shape((4, length, hdim), BF16)],
        in_specs=[SMEM, SMEM, VMEM, VMEM, VMEM],
        out_specs=[VMEM] * 2,
        scratch_shapes=[pltpu.VMEM((2, 2 * length, hdim), F32), pltpu.SMEM((pools,), jnp.int32)],
        compiler_params=params(60),
        cost_estimate=pl.CostEstimate(flops=0, bytes_accessed=3_000_000, transcendentals=0),
        name="dispatch",
    )(row_prefix, owner_map, queries, prefix_keys.reshape(-1, hdim), prefix_values.reshape(-1, hdim))

    arrived = lax.all_to_all(
        outgoing.reshape(pools, CAP, heads, hdim), "pool", split_axis=0, concat_axis=0, tiled=True
    ).reshape(slots, heads, hdim)
    mirror = [ring - 1 - i for i in range(ring)]
    asked = meet(arrived, "y", mirror)

    pair = meet(own, "y", [i ^ 1 for i in range(ring)])
    pair, arrived_later = lax.optimization_barrier((pair, arrived))
    blocks = {
        (0, 0): own,
        (0, 1): meet(own, "core", [1, 0]),
        (1, 0): pair,
        (1, 1): meet(pair, "core", [1, 0]),
    }

    def attend(q, *sources):
        span = len(sources) * length
        return pl.pallas_call(
            functools.partial(attend_kernel, sources),
            out_shape=shape((slots + 3, heads, hdim), BF16),
            in_specs=[SMEM, SMEM, VMEM] + [VMEM] * len(sources),
            out_specs=VMEM,
            compiler_params=params(30),
            cost_estimate=pl.CostEstimate(
                flops=6 * slots * heads * span * hdim,
                bytes_accessed=3_000_000,
                transcendentals=slots * heads * span,
            ),
            name="attend",
        )(owner_map, prefix_lengths, q, *(blocks[source] for source in sources))

    near, far = ((0, 0), (0, 1)), ((1, 0), (1, 1))
    near_part, asked = lax.optimization_barrier((attend(arrived, *near), asked))
    answer = meet(attend(asked, *near, *far), "y", mirror)
    far_part = attend(arrived_later, *far)
    merged = pl.pallas_call(
        merge_kernel,
        out_shape=shape((pools * (CAP * heads + GROUP), hdim), BF16),
        in_specs=[VMEM] * 3,
        out_specs=VMEM,
        compiler_params=params(8),
        cost_estimate=pl.CostEstimate(flops=0, bytes_accessed=1_000_000, transcendentals=0),
        name="merge",
    )(near_part, far_part, answer)
    merged, queries_later = lax.optimization_barrier((merged, queries))
    returned = lax.all_to_all(
        merged.reshape(pools, CAP * heads + GROUP, hdim),
        "pool",
        split_axis=0,
        concat_axis=0,
        tiled=True,
    ).reshape(-1, hdim)

    suffix_out, suffix_lse = pl.pallas_call(
        suffix_kernel,
        out_shape=[shape((rows, heads, hdim), F32)] * 2,
        in_specs=[SMEM, VMEM, VMEM, VMEM],
        out_specs=[VMEM] * 2,
        compiler_params=params(8),
        cost_estimate=pl.CostEstimate(
            flops=4 * rows * heads * 128 * 128, bytes_accessed=2_000_000, transcendentals=0
        ),
        name="suffix",
    )(
        suffix_lengths,
        queries_later,
        suffix_keys.reshape(rows, -1, hdim),
        suffix_values.reshape(rows, -1, hdim),
    )

    attended = pl.pallas_call(
        combine_kernel,
        out_shape=shape((2 * ring, rows, heads * hdim), BF16),
        in_specs=[SMEM, SMEM, VMEM, VMEM, VMEM],
        out_specs=VMEM,
        scratch_shapes=[
            pltpu.VMEM((pools * (CAP * heads + GROUP), hdim), F32),
            pltpu.VMEM((rows * heads, hdim), F32),
            pltpu.SMEM((pools,), jnp.int32),
        ],
        compiler_params=params(60),
        cost_estimate=pl.CostEstimate(flops=0, bytes_accessed=1_000_000, transcendentals=0),
        name="combine",
    )(row_prefix, owner_map, returned, suffix_out, suffix_lse)
    gathered = lax.all_to_all(attended, ("y", "core"), split_axis=0, concat_axis=0, tiled=True)
    terms = pl.pallas_call(
        project_kernel,
        out_shape=shape((2 * ring * rows, columns), BF16),
        in_specs=[VMEM] * 2,
        out_specs=VMEM,
        compiler_params=params(16),
        cost_estimate=pl.CostEstimate(
            flops=4 * ring * rows * heads * hdim * columns,
            bytes_accessed=4_000_000,
            transcendentals=0,
        ),
        name="project",
    )(gathered.reshape(-1, heads * hdim), out_weight)
    shared = lax.all_to_all(
        terms.reshape(lax.axis_size("head"), -1, columns), "head", split_axis=0, concat_axis=0, tiled=True
    )
    return jnp.sum(shared.astype(F32), axis=0).astype(BF16)


def solution(mesh):
    pools, across, groups = mesh.devices.shape
    fine = Mesh(
        mesh.devices.reshape(pools, across // 2, 2, groups), ("pool", "y", "core", "head")
    )
    row = ("y", "core")
    every = ("pool", "y", "core")
    return jax.shard_map(
        body,
        mesh=fine,
        in_specs=(
            P(every, "head", None),
            P("pool", row, "head", None),
            P("pool", row, "head", None),
            P(every, None, "head", None),
            P(every, None, "head", None),
            P(every, None),
            P(),
            P(),
            P(every),
            P("head", row),
        ),
        out_specs=P(("pool", "head"), row),
        check_vma=False,
    )
```

```python
import functools
import math

import jax
import jax.numpy as jnp
from jax import lax
from jax.experimental import pallas as pl
from jax.experimental.pallas import tpu as pltpu
from jax.sharding import Mesh, PartitionSpec as P

LOWEST = -1e30
CAP = 3
GROUP = 8
HD = 128
SCALE = HD**-0.5
LOG2E = math.log2(math.e)
F32 = jnp.float32
BF16 = jnp.bfloat16

VMEM = pl.BlockSpec(memory_space=pltpu.VMEM)
HBM = pl.BlockSpec(memory_space=pltpu.HBM)
TAIL = 16


def params(mib):
    return pltpu.CompilerParams(vmem_limit_bytes=mib * 1024 * 1024)


def split3(value):
    high = value.astype(BF16).astype(F32)
    rest = value - high
    middle = rest.astype(BF16).astype(F32)
    return high, middle, (rest - middle).astype(BF16).astype(F32)


def slot_of(row, row_prefix_ref, owner_ref, count_ref):
    owner = owner_ref[row_prefix_ref[row]]
    place = count_ref[owner]
    count_ref[owner] = place + 1
    return owner, place


def fetch(pairs, sems):
    copies = [pltpu.make_async_copy(*pair, sems.at[i]) for i, pair in enumerate(pairs)]
    for copy in copies:
        copy.start()
    return copies


def dispatch_kernel(
    row_prefix_hbm, owner_hbm, lengths_hbm, q_hbm, k_hbm, v_hbm, out_ref, block_ref,
    row_prefix_ref, owner_ref, lengths_ref, q_ref, mixed, held, count_ref, sems,
):
    copies = fetch(
        (
            (row_prefix_hbm, row_prefix_ref),
            (owner_hbm, owner_ref),
            (lengths_hbm, lengths_ref),
            (q_hbm, q_ref),
            (k_hbm, mixed.at[0]),
            (v_hbm, mixed.at[1]),
        ),
        sems,
    )
    pools = owner_ref.shape[0]
    length = mixed.shape[1] // 2
    for p in range(pools):
        count_ref[p] = 0
    out_ref[...] = jnp.zeros_like(out_ref)
    for copy in copies[:4]:
        copy.wait()
    for r in range(q_ref.shape[0]):
        owner, place = slot_of(r, row_prefix_ref, owner_ref, count_ref)
        out_ref[owner * CAP + place] = q_ref[r]
    pool = lax.axis_index("pool")
    seen = -(lax.axis_index("y") * 2 + lax.axis_index("core")) * length
    for p in range(pools):
        seen += jnp.where(owner_ref[p] == pool, lengths_ref[p], 0)
    tail = (TAIL, HD)
    token = lax.broadcasted_iota(jnp.int32, tail, 0) * HD + lax.broadcasted_iota(jnp.int32, tail, 1)
    block_ref[pl.ds(4 * length, TAIL), :] = jnp.where(token < seen, 0.0, LOWEST).astype(BF16)
    for n in range(2):
        copies[4 + n].wait()
        held[n] = mixed[n].astype(F32)
        for g in range(2):
            block_ref[pl.ds((2 * n + g) * length, length), :] = held[
                n, pl.ds(g, length, stride=2), :
            ].astype(BF16)


def attend_kernel(q_ref, *refs):
    blocks, out_ref = refs[:-1], refs[-1]
    slots = q_ref.shape[0]
    step_slots = math.gcd(24, slots)
    length = (blocks[0].shape[0] - TAIL) // 4
    width = min(512, length)
    units = [(start, g) for start in range(0, slots, step_slots) for g in range(2)]
    pieces = [(block, at) for block in blocks for at in range(0, length, width)]
    lane = lax.broadcasted_iota(jnp.int32, (GROUP, 128), 1)
    ones = jnp.ones((width, HD), BF16)
    tails = [block[pl.ds(4 * length, TAIL), :].astype(F32) for block in blocks]
    biases = [
        jnp.concatenate(
            [tail[row : row + 1] for row in range(at // HD, (at + width) // HD)], axis=1
        )
        for tail in tails
        for at in range(0, length, width)
    ]

    def query(unit):
        start, g = unit
        held = q_ref[pl.ds(start, step_slots)].astype(F32)[:, g * GROUP : (g + 1) * GROUP, :]
        return held.reshape(step_slots * GROUP, HD).astype(BF16)

    def score(q, g, n):
        block, at = pieces[n]
        keys = block[pl.ds(g * length + at, width), :]
        return (
            lax.dot_general(q, keys, (((1,), (1,)), ((), ())), preferred_element_type=F32)
            + biases[n]
        )

    packed = [jnp.zeros((GROUP, 128), F32)] * 2
    kept = {}
    q = query(units[0])
    scores = [score(q, units[0][1], n) for n in range(len(pieces))]
    for i, (start, g) in enumerate(units):
        peak = functools.reduce(
            jnp.maximum, [jnp.max(part, axis=1, keepdims=True) for part in scores]
        )
        peak = jnp.maximum(peak, 0.1 * LOWEST)
        coming = []
        both = None
        if i + 1 < len(units):
            q = query(units[i + 1])
        for n, (block, at) in enumerate(pieces):
            weights = jnp.exp2((scores[n] - peak) * (SCALE * LOG2E)).astype(BF16)
            if i + 1 < len(units):
                coming.append(score(q, units[i + 1][1], n))
            values = jnp.concatenate(
                [block[pl.ds((2 + g) * length + at, width), :], ones], axis=1
            )
            term = jnp.dot(weights, values, preferred_element_type=F32)
            both = term if both is None else both + term
        scores = coming
        total = both[:, HD:]
        live = total > 0
        safe = jnp.where(live, total, 1.0)
        kept[g] = (both[:, :HD] / safe).reshape(step_slots, GROUP, HD)
        lse = jnp.where(live, peak * SCALE + jnp.log(safe), LOWEST)
        lse = lse.reshape(step_slots, GROUP, HD)
        for s in range(step_slots):
            packed[g] = jnp.where(lane == start + s, lse[s], packed[g])
        if g == 1:
            out_ref[pl.ds(start, step_slots)] = jnp.concatenate(
                [kept[0], kept[1]], axis=1
            ).astype(BF16)
    for i, plane in enumerate(split3(jnp.concatenate(packed, axis=0))):
        out_ref[slots + i] = plane.astype(BF16)


def merge_kernel(a_ref, b_ref, c_ref, out_ref):
    blocks = (a_ref, b_ref, c_ref)
    slots = a_ref.shape[0] - 3
    pools = slots // CAP
    lses = [
        (ref[slots + 2].astype(F32) + ref[slots + 1].astype(F32)) + ref[slots].astype(F32)
        for ref in blocks
    ]
    top = functools.reduce(jnp.maximum, lses)
    shares = [jnp.exp(lse - top) for lse in lses]
    total = functools.reduce(jnp.add, shares)
    weights = [share / total for share in shares]
    planes = split3(top + jnp.log(total))
    lane = lax.broadcasted_iota(jnp.int32, (GROUP, 128), 1)
    for pair in range(0, pools, 2):
        rows = []
        for p in (pair, pair + 1):
            for s in range(p * CAP, (p + 1) * CAP):
                terms = [
                    weight[:, s : s + 1] * ref[s].astype(F32) for weight, ref in zip(weights, blocks)
                ]
                rows.append(functools.reduce(jnp.add, terms))
            tile = jnp.zeros((GROUP, 128), F32)
            for i, plane in enumerate(planes):
                for g in range(2):
                    at = i * 16 + g * 8
                    moved = plane[g * GROUP : (g + 1) * GROUP]
                    shift = (at - p * CAP) % 128
                    if shift:
                        moved = pltpu.roll(moved, shift, 1)
                    tile = jnp.where((lane >= at) & (lane < at + CAP), moved, tile)
            rows.append(tile)
        height = CAP * 16 + GROUP
        out_ref[pl.ds(pair * height, 2 * height), :] = jnp.concatenate(rows, axis=0).astype(BF16)


def suffix_kernel(length_hbm, q_ref, k_ref, v_ref, out_ref, lse_ref, length_ref, sems):
    fetch(((length_hbm, length_ref),), sems)[0].wait()
    span = k_ref.shape[1]
    column = lax.broadcasted_iota(jnp.int32, (2 * GROUP, span), 1)
    head = lax.broadcasted_iota(jnp.int32, (2 * GROUP, span), 0)
    same = (column & 1) == head // GROUP
    for r in range(q_ref.shape[0]):
        scores = lax.dot_general(
            q_ref[r], k_ref[r], (((1,), (1,)), ((), ())), preferred_element_type=F32
        )
        visible = same & (column < 2 * length_ref[r])
        scores = jnp.where(visible, scores * SCALE, LOWEST)
        peak = jnp.max(scores, axis=1, keepdims=True)
        powers = jnp.exp(scores - peak)
        total = jnp.sum(powers, axis=1, keepdims=True)
        summed = jnp.dot(powers.astype(BF16), v_ref[r], preferred_element_type=F32)
        out_ref[r] = summed / total
        lse_ref[r] = jnp.broadcast_to(peak + jnp.log(total), (2 * GROUP, HD))


def combine_kernel(
    row_prefix_hbm, owner_hbm, got_ref, suffix_hbm, suffix_lse_hbm, out_ref,
    row_prefix_ref, owner_ref, suffix_ref, suffix_lse_ref, wide, mixed, count_ref, sems,
):
    copies = fetch(
        (
            (row_prefix_hbm, row_prefix_ref),
            (owner_hbm, owner_ref),
            (suffix_hbm, suffix_ref),
            (suffix_lse_hbm, suffix_lse_ref),
        ),
        sems,
    )
    rows = suffix_ref.shape[0]
    height = CAP * 16 + GROUP
    for p in range(owner_ref.shape[0]):
        count_ref[p] = 0
    wide[...] = got_ref[...].astype(F32)
    for copy in copies:
        copy.wait()
    lane = lax.broadcasted_iota(jnp.int32, (GROUP, 128), 1)
    for r in range(rows):
        owner, place = slot_of(r, row_prefix_ref, owner_ref, count_ref)
        base = owner * height
        prefix = wide[pl.ds(pl.multiple_of(base + place * 16, 8), 16), :]
        tile = wide[pl.ds(pl.multiple_of(base + CAP * 16, 8), GROUP), :]
        lses = []
        for g in range(2):
            chosen = ((lane & 15) == place + g * 8) & (lane < 48)
            lses.append(jnp.sum(jnp.where(chosen, tile, 0.0), axis=1, keepdims=True))
        prefix_lse = jnp.broadcast_to(jnp.concatenate(lses, axis=0), (2 * GROUP, HD))
        suffix_lse = suffix_lse_ref[r]
        highest = jnp.maximum(prefix_lse, suffix_lse)
        a = jnp.exp(prefix_lse - highest)
        b = jnp.exp(suffix_lse - highest)
        mixed[r * 16 : (r + 1) * 16, :] = (a * prefix + b * suffix_ref[r]) / (a + b)
    for h in range(2 * GROUP):
        piece = mixed[pl.ds(h, rows, stride=16), :].astype(BF16)
        for n in range(out_ref.shape[0]):
            out_ref[n, :, h * HD : (h + 1) * HD] = piece


def project_kernel(own_ref, other_ref, w_ref, out_ref):
    count, rows, depth = own_ref.shape
    core = lax.axis_index("core")
    both = jnp.concatenate(
        [own_ref[...].reshape(count * rows, depth), other_ref[...].reshape(count * rows, depth)],
        axis=0,
    )
    terms = jnp.dot(both, w_ref[...], preferred_element_type=F32).astype(BF16)
    terms = terms.reshape(2, count, rows, -1)
    for n in range(count):
        out_ref[n, core] = terms[0, n]
        out_ref[n, 1 - core] = terms[1, n]


def body(
    queries,
    prefix_keys,
    prefix_values,
    suffix_keys,
    suffix_values,
    row_prefix,
    owner_map,
    prefix_lengths,
    suffix_lengths,
    out_weight,
):
    rows, heads, hdim = queries.shape
    row_prefix = row_prefix.reshape(-1)
    pools = lax.axis_size("pool")
    ring = lax.axis_size("y")
    slots = pools * CAP
    columns = out_weight.shape[1]
    shape = jax.ShapeDtypeStruct

    def meet(value, axis, apart):
        pairs = [(i, i ^ apart) for i in range(lax.axis_size(axis))]
        return lax.ppermute(value, axis, pairs)

    def ints(count):
        return pltpu.SMEM((count,), jnp.int32)

    length = prefix_keys.shape[1]
    outgoing, own = pl.pallas_call(
        dispatch_kernel,
        out_shape=[shape((slots, heads, hdim), BF16), shape((4 * length + TAIL, hdim), BF16)],
        in_specs=[HBM] * 6,
        out_specs=[VMEM] * 2,
        scratch_shapes=[
            ints(rows),
            ints(pools),
            ints(pools),
            pltpu.VMEM((rows, heads, hdim), BF16),
            pltpu.VMEM((2, 2 * length, hdim), BF16),
            pltpu.VMEM((2, 2 * length, hdim), F32),
            ints(pools),
            pltpu.SemaphoreType.DMA((6,)),
        ],
        compiler_params=params(60),
        cost_estimate=pl.CostEstimate(flops=0, bytes_accessed=3_000_000, transcendentals=0),
        name="dispatch",
    )(
        row_prefix,
        owner_map,
        prefix_lengths,
        queries,
        prefix_keys.reshape(-1, hdim),
        prefix_values.reshape(-1, hdim),
    )

    arrived = lax.all_to_all(
        outgoing.reshape(pools, CAP, heads, hdim), "pool", split_axis=0, concat_axis=0, tiled=True
    ).reshape(slots, heads, hdim)
    asked = meet(arrived, "y", 3)

    blocks = {(0, 0): own, (0, 1): meet(own, "core", 1), (1, 0): meet(own, "y", 1)}

    def attend(q, *sources):
        span = len(sources) * length
        return pl.pallas_call(
            attend_kernel,
            out_shape=shape((slots + 3, heads, hdim), BF16),
            in_specs=[VMEM] * (1 + len(sources)),
            out_specs=VMEM,
            compiler_params=params(30),
            cost_estimate=pl.CostEstimate(
                flops=6 * slots * heads * span * hdim,
                bytes_accessed=3_000_000,
                transcendentals=slots * heads * span,
            ),
            name="attend",
        )(q, *(blocks[source] for source in sources))

    near, far = ((0, 0), (0, 1)), ((1, 0), (1, 1))
    near_part, blocks[1, 0] = lax.optimization_barrier(
        (attend(arrived, *near), blocks[1, 0])
    )
    blocks[1, 1] = meet(blocks[1, 0], "core", 1)
    answer = meet(attend(asked, *near, *far), "y", 3)
    far_part = attend(arrived, *far)
    merged = pl.pallas_call(
        merge_kernel,
        out_shape=shape((pools * (CAP * heads + GROUP), hdim), BF16),
        in_specs=[VMEM] * 3,
        out_specs=VMEM,
        compiler_params=params(8),
        cost_estimate=pl.CostEstimate(flops=0, bytes_accessed=1_000_000, transcendentals=0),
        name="merge",
    )(near_part, far_part, answer)
    merged, queries_later = lax.optimization_barrier((merged, queries))
    returned = lax.all_to_all(
        merged.reshape(pools, CAP * heads + GROUP, hdim),
        "pool",
        split_axis=0,
        concat_axis=0,
        tiled=True,
    ).reshape(-1, hdim)

    suffix_out, suffix_lse = pl.pallas_call(
        suffix_kernel,
        out_shape=[shape((rows, heads, hdim), F32)] * 2,
        in_specs=[HBM, VMEM, VMEM, VMEM],
        out_specs=[VMEM] * 2,
        scratch_shapes=[ints(rows), pltpu.SemaphoreType.DMA((1,))],
        compiler_params=params(8),
        cost_estimate=pl.CostEstimate(
            flops=4 * rows * heads * 128 * 128, bytes_accessed=2_000_000, transcendentals=0
        ),
        name="suffix",
    )(
        suffix_lengths,
        queries_later,
        suffix_keys.reshape(rows, -1, hdim),
        suffix_values.reshape(rows, -1, hdim),
    )

    attended = pl.pallas_call(
        combine_kernel,
        out_shape=shape((ring, rows, heads * hdim), BF16),
        in_specs=[HBM, HBM, VMEM, HBM, HBM],
        out_specs=VMEM,
        scratch_shapes=[
            ints(rows),
            ints(pools),
            pltpu.VMEM((rows, heads, hdim), F32),
            pltpu.VMEM((rows, heads, hdim), F32),
            pltpu.VMEM((pools * (CAP * heads + GROUP), hdim), F32),
            pltpu.VMEM((rows * heads, hdim), F32),
            ints(pools),
            pltpu.SemaphoreType.DMA((4,)),
        ],
        compiler_params=params(8),
        cost_estimate=pl.CostEstimate(flops=0, bytes_accessed=1_000_000, transcendentals=0),
        name="combine",
    )(row_prefix, owner_map, returned, suffix_out, suffix_lse)
    gathered = lax.all_to_all(attended, "y", split_axis=0, concat_axis=0, tiled=True)
    terms = pl.pallas_call(
        project_kernel,
        out_shape=shape((ring, 2, rows, columns), BF16),
        in_specs=[VMEM] * 3,
        out_specs=VMEM,
        compiler_params=params(16),
        cost_estimate=pl.CostEstimate(
            flops=4 * ring * rows * heads * hdim * columns,
            bytes_accessed=4_000_000,
            transcendentals=0,
        ),
        name="project",
    )(gathered, meet(gathered, "core", 1), out_weight)
    shared = lax.all_to_all(
        terms.reshape(lax.axis_size("head"), -1, columns),
        "head",
        split_axis=0,
        concat_axis=0,
        tiled=True,
    )
    return jnp.sum(shared.astype(F32), axis=0).astype(BF16)


def solution(mesh):
    pools, across, groups = mesh.devices.shape
    fine = Mesh(
        mesh.devices.reshape(pools, across // 2, 2, groups), ("pool", "y", "core", "head")
    )
    row = ("y", "core")
    every = ("pool", "y", "core")
    return jax.shard_map(
        body,
        mesh=fine,
        in_specs=(
            P(every, "head", None),
            P("pool", row, "head", None),
            P("pool", row, "head", None),
            P(every, None, "head", None),
            P(every, None, "head", None),
            P(every, None),
            P(),
            P(),
            P(every),
            P("head", row),
        ),
        out_specs=P(("pool", "head"), row),
        check_vma=False,
    )
```

```python
import functools
import math

import jax
import jax.numpy as jnp
from jax import lax
from jax.experimental import pallas as pl
from jax.experimental.pallas import tpu as pltpu
from jax.sharding import Mesh, PartitionSpec as P

LOWEST = -1e30
CAP = 3
GROUP = 8
HD = 128
SCALE = HD**-0.5
LOG2E = math.log2(math.e)
F32 = jnp.float32
BF16 = jnp.bfloat16

VMEM = pl.BlockSpec(memory_space=pltpu.VMEM)
HBM = pl.BlockSpec(memory_space=pltpu.HBM)
TAIL = 16


def params(mib):
    return pltpu.CompilerParams(vmem_limit_bytes=mib * 1024 * 1024)


def split3(value):
    high = value.astype(BF16).astype(F32)
    rest = value - high
    middle = rest.astype(BF16).astype(F32)
    return high, middle, (rest - middle).astype(BF16).astype(F32)


def slot_of(row, row_prefix_ref, owner_ref, count_ref):
    owner = owner_ref[row_prefix_ref[row]]
    place = count_ref[owner]
    count_ref[owner] = place + 1
    return owner, place


def fetch(pairs, sems):
    copies = [pltpu.make_async_copy(*pair, sems.at[i]) for i, pair in enumerate(pairs)]
    for copy in copies:
        copy.start()
    return copies


def dispatch_kernel(
    row_prefix_hbm, owner_hbm, lengths_hbm, q_hbm, k_hbm, v_hbm, out_ref, block_ref,
    row_prefix_ref, owner_ref, lengths_ref, q_ref, mixed, held, count_ref, sems,
):
    copies = fetch(
        (
            (row_prefix_hbm, row_prefix_ref),
            (owner_hbm, owner_ref),
            (lengths_hbm, lengths_ref),
            (q_hbm, q_ref),
            (k_hbm, mixed.at[0]),
            (v_hbm, mixed.at[1]),
        ),
        sems,
    )
    pools = owner_ref.shape[0]
    length = mixed.shape[1] // 2
    for p in range(pools):
        count_ref[p] = 0
    out_ref[...] = jnp.zeros_like(out_ref)
    for copy in copies[:4]:
        copy.wait()
    for r in range(q_ref.shape[0]):
        owner, place = slot_of(r, row_prefix_ref, owner_ref, count_ref)
        out_ref[owner * CAP + place] = q_ref[r]
    pool = lax.axis_index("pool")
    seen = -(lax.axis_index("y") * 2 + lax.axis_index("core")) * length
    for p in range(pools):
        seen += jnp.where(owner_ref[p] == pool, lengths_ref[p], 0)
    tail = (TAIL, HD)
    token = lax.broadcasted_iota(jnp.int32, tail, 0) * HD + lax.broadcasted_iota(jnp.int32, tail, 1)
    block_ref[pl.ds(4 * length, TAIL), :] = jnp.where(token < seen, 0.0, LOWEST).astype(BF16)
    for n in range(2):
        copies[4 + n].wait()
        held[n] = mixed[n].astype(F32)
        for g in range(2):
            block_ref[pl.ds((2 * n + g) * length, length), :] = held[
                n, pl.ds(g, length, stride=2), :
            ].astype(BF16)


def attend_kernel(q_ref, *refs):
    blocks, out_ref = refs[:-1], refs[-1]
    slots = q_ref.shape[0]
    step_slots = math.gcd(24, slots)
    length = (blocks[0].shape[0] - TAIL) // 4
    width = min(512, length)
    units = [(start, g) for start in range(0, slots, step_slots) for g in range(2)]
    pieces = [(block, at) for block in blocks for at in range(0, length, width)]
    lane = lax.broadcasted_iota(jnp.int32, (GROUP, 128), 1)
    ones = jnp.ones((width, HD), BF16)
    tails = [block[pl.ds(4 * length, TAIL), :].astype(F32) for block in blocks]
    biases = [
        jnp.concatenate(
            [tail[row : row + 1] for row in range(at // HD, (at + width) // HD)], axis=1
        )
        for tail in tails
        for at in range(0, length, width)
    ]

    def query(unit):
        start, g = unit
        held = q_ref[pl.ds(start, step_slots)].astype(F32)[:, g * GROUP : (g + 1) * GROUP, :]
        return held.reshape(step_slots * GROUP, HD).astype(BF16)

    def score(q, g, n):
        block, at = pieces[n]
        keys = block[pl.ds(g * length + at, width), :]
        return (
            lax.dot_general(q, keys, (((1,), (1,)), ((), ())), preferred_element_type=F32)
            + biases[n]
        )

    packed = [jnp.zeros((GROUP, 128), F32)] * 2
    kept = {}
    q = query(units[0])
    scores = [score(q, units[0][1], n) for n in range(len(pieces))]
    for i, (start, g) in enumerate(units):
        peak = functools.reduce(
            jnp.maximum, [jnp.max(part, axis=1, keepdims=True) for part in scores]
        )
        peak = jnp.maximum(peak, 0.1 * LOWEST)
        coming = []
        both = None
        if i + 1 < len(units):
            q = query(units[i + 1])
        for n, (block, at) in enumerate(pieces):
            weights = jnp.exp2((scores[n] - peak) * (SCALE * LOG2E)).astype(BF16)
            if i + 1 < len(units):
                coming.append(score(q, units[i + 1][1], n))
            values = jnp.concatenate(
                [block[pl.ds((2 + g) * length + at, width), :], ones], axis=1
            )
            term = jnp.dot(weights, values, preferred_element_type=F32)
            both = term if both is None else both + term
        scores = coming
        total = both[:, HD:]
        live = total > 0
        safe = jnp.where(live, total, 1.0)
        kept[g] = (both[:, :HD] / safe).reshape(step_slots, GROUP, HD)
        lse = jnp.where(live, peak * SCALE + jnp.log(safe), LOWEST)
        lse = lse.reshape(step_slots, GROUP, HD)
        for s in range(step_slots):
            packed[g] = jnp.where(lane == start + s, lse[s], packed[g])
        if g == 1:
            out_ref[pl.ds(start, step_slots)] = jnp.concatenate(
                [kept[0], kept[1]], axis=1
            ).astype(BF16)
    for i, plane in enumerate(split3(jnp.concatenate(packed, axis=0))):
        out_ref[slots + i] = plane.astype(BF16)


def merge_kernel(a_ref, b_ref, c_ref, out_ref):
    blocks = (a_ref, b_ref, c_ref)
    slots = a_ref.shape[0] - 3
    pools = slots // CAP
    lses = [
        (ref[slots + 2].astype(F32) + ref[slots + 1].astype(F32)) + ref[slots].astype(F32)
        for ref in blocks
    ]
    top = functools.reduce(jnp.maximum, lses)
    shares = [jnp.exp(lse - top) for lse in lses]
    total = functools.reduce(jnp.add, shares)
    weights = [share / total for share in shares]
    planes = split3(top + jnp.log(total))
    lane = lax.broadcasted_iota(jnp.int32, (GROUP, 128), 1)
    for pair in range(0, pools, 2):
        rows = []
        for p in (pair, pair + 1):
            for s in range(p * CAP, (p + 1) * CAP):
                terms = [
                    weight[:, s : s + 1] * ref[s].astype(F32) for weight, ref in zip(weights, blocks)
                ]
                rows.append(functools.reduce(jnp.add, terms))
            tile = jnp.zeros((GROUP, 128), F32)
            for i, plane in enumerate(planes):
                for g in range(2):
                    at = i * 16 + g * 8
                    moved = plane[g * GROUP : (g + 1) * GROUP]
                    shift = (at - p * CAP) % 128
                    if shift:
                        moved = pltpu.roll(moved, shift, 1)
                    tile = jnp.where((lane >= at) & (lane < at + CAP), moved, tile)
            rows.append(tile)
        height = CAP * 16 + GROUP
        out_ref[pl.ds(pair * height, 2 * height), :] = jnp.concatenate(rows, axis=0).astype(BF16)


def suffix_kernel(length_hbm, q_ref, k_ref, v_ref, out_ref, length_ref, sems):
    fetch(((length_hbm, length_ref),), sems)[0].wait()
    span = k_ref.shape[1]
    column = lax.broadcasted_iota(jnp.int32, (2 * GROUP, span), 1)
    head = lax.broadcasted_iota(jnp.int32, (2 * GROUP, span), 0)
    same = (column & 1) == head // GROUP
    for r in range(q_ref.shape[0]):
        scores = lax.dot_general(
            q_ref[r], k_ref[r], (((1,), (1,)), ((), ())), preferred_element_type=F32
        )
        visible = same & (column < 2 * length_ref[r])
        scores = jnp.where(visible, scores * SCALE, LOWEST)
        peak = jnp.max(scores, axis=1, keepdims=True)
        powers = jnp.exp(scores - peak)
        total = jnp.sum(powers, axis=1, keepdims=True)
        summed = jnp.dot(powers.astype(BF16), v_ref[r], preferred_element_type=F32)
        out_ref[r, : 2 * GROUP] = summed / total
        out_ref[r, 2 * GROUP :] = jnp.broadcast_to(peak + jnp.log(total), (2 * GROUP, HD))


def combine_kernel(
    row_prefix_hbm, owner_hbm, got_ref, suffix_hbm, out_ref,
    row_prefix_ref, owner_ref, suffix_ref, wide, mixed, count_ref, sems,
):
    copies = fetch(
        (
            (row_prefix_hbm, row_prefix_ref),
            (owner_hbm, owner_ref),
            (suffix_hbm, suffix_ref),
        ),
        sems,
    )
    rows = suffix_ref.shape[0]
    height = CAP * 16 + GROUP
    for p in range(owner_ref.shape[0]):
        count_ref[p] = 0
    wide[...] = got_ref[...].astype(F32)
    for copy in copies:
        copy.wait()
    lane = lax.broadcasted_iota(jnp.int32, (GROUP, 128), 1)
    for r in range(rows):
        owner, place = slot_of(r, row_prefix_ref, owner_ref, count_ref)
        base = owner * height
        prefix = wide[pl.ds(pl.multiple_of(base + place * 16, 8), 16), :]
        tile = wide[pl.ds(pl.multiple_of(base + CAP * 16, 8), GROUP), :]
        lses = []
        for g in range(2):
            chosen = ((lane & 15) == place + g * 8) & (lane < 48)
            lses.append(jnp.sum(jnp.where(chosen, tile, 0.0), axis=1, keepdims=True))
        prefix_lse = jnp.broadcast_to(jnp.concatenate(lses, axis=0), (2 * GROUP, HD))
        suffix_lse = suffix_ref[r, 2 * GROUP :]
        highest = jnp.maximum(prefix_lse, suffix_lse)
        a = jnp.exp(prefix_lse - highest)
        b = jnp.exp(suffix_lse - highest)
        mixed[r * 16 : (r + 1) * 16, :] = (a * prefix + b * suffix_ref[r, : 2 * GROUP]) / (a + b)
    for h in range(2 * GROUP):
        piece = mixed[pl.ds(h, rows, stride=16), :].astype(BF16)
        for n in range(out_ref.shape[0]):
            out_ref[n, :, h * HD : (h + 1) * HD] = piece


def project_kernel(own_ref, other_ref, w_ref, out_ref):
    count, rows, depth = own_ref.shape
    core = lax.axis_index("core")
    both = jnp.concatenate(
        [own_ref[...].reshape(count * rows, depth), other_ref[...].reshape(count * rows, depth)],
        axis=0,
    )
    terms = jnp.dot(both, w_ref[...], preferred_element_type=F32).astype(BF16)
    terms = terms.reshape(2, count, rows, -1)
    for n in range(count):
        out_ref[n, core] = terms[0, n]
        out_ref[n, 1 - core] = terms[1, n]


def body(
    queries,
    prefix_keys,
    prefix_values,
    suffix_keys,
    suffix_values,
    row_prefix,
    owner_map,
    prefix_lengths,
    suffix_lengths,
    out_weight,
):
    rows, heads, hdim = queries.shape
    row_prefix = row_prefix.reshape(-1)
    pools = lax.axis_size("pool")
    ring = lax.axis_size("y")
    slots = pools * CAP
    columns = out_weight.shape[1]
    shape = jax.ShapeDtypeStruct

    def meet(value, axis, apart):
        pairs = [(i, i ^ apart) for i in range(lax.axis_size(axis))]
        return lax.ppermute(value, axis, pairs)

    def ints(count):
        return pltpu.SMEM((count,), jnp.int32)

    length = prefix_keys.shape[1]
    outgoing, own = pl.pallas_call(
        dispatch_kernel,
        out_shape=[shape((slots, heads, hdim), BF16), shape((4 * length + TAIL, hdim), BF16)],
        in_specs=[HBM] * 6,
        out_specs=[VMEM] * 2,
        scratch_shapes=[
            ints(rows),
            ints(pools),
            ints(pools),
            pltpu.VMEM((rows, heads, hdim), BF16),
            pltpu.VMEM((2, 2 * length, hdim), BF16),
            pltpu.VMEM((2, 2 * length, hdim), F32),
            ints(pools),
            pltpu.SemaphoreType.DMA((6,)),
        ],
        compiler_params=params(60),
        cost_estimate=pl.CostEstimate(flops=0, bytes_accessed=3_000_000, transcendentals=0),
        name="dispatch",
    )(
        row_prefix,
        owner_map,
        prefix_lengths,
        queries,
        prefix_keys.reshape(-1, hdim),
        prefix_values.reshape(-1, hdim),
    )

    arrived = lax.all_to_all(
        outgoing.reshape(pools, CAP, heads, hdim), "pool", split_axis=0, concat_axis=0, tiled=True
    ).reshape(slots, heads, hdim)
    asked = meet(arrived, "y", 1)

    pair, arrived_later = lax.optimization_barrier((meet(own, "y", 3), arrived))
    blocks = {(0, 0): own, (0, 1): meet(own, "core", 1), (1, 0): pair, (1, 1): meet(pair, "core", 1)}

    def attend(q, *sources):
        span = len(sources) * length
        return pl.pallas_call(
            attend_kernel,
            out_shape=shape((slots + 3, heads, hdim), BF16),
            in_specs=[VMEM] * (1 + len(sources)),
            out_specs=VMEM,
            compiler_params=params(30),
            cost_estimate=pl.CostEstimate(
                flops=6 * slots * heads * span * hdim,
                bytes_accessed=3_000_000,
                transcendentals=slots * heads * span,
            ),
            name="attend",
        )(q, *(blocks[source] for source in sources))

    near, far = ((0, 0), (0, 1)), ((1, 0), (1, 1))
    near_part, asked = lax.optimization_barrier((attend(arrived, *near), asked))
    answer = meet(attend(asked, *near, *far), "y", 1)
    far_part = attend(arrived_later, *far)
    merged = pl.pallas_call(
        merge_kernel,
        out_shape=shape((pools * (CAP * heads + GROUP), hdim), BF16),
        in_specs=[VMEM] * 3,
        out_specs=VMEM,
        compiler_params=params(8),
        cost_estimate=pl.CostEstimate(flops=0, bytes_accessed=1_000_000, transcendentals=0),
        name="merge",
    )(near_part, far_part, answer)
    merged, queries_later = lax.optimization_barrier((merged, queries))
    returned = lax.all_to_all(
        merged.reshape(pools, CAP * heads + GROUP, hdim),
        "pool",
        split_axis=0,
        concat_axis=0,
        tiled=True,
    ).reshape(-1, hdim)

    suffix = pl.pallas_call(
        suffix_kernel,
        out_shape=shape((rows, 2 * heads, hdim), F32),
        in_specs=[HBM, VMEM, VMEM, VMEM],
        out_specs=VMEM,
        scratch_shapes=[ints(rows), pltpu.SemaphoreType.DMA((1,))],
        compiler_params=params(8),
        cost_estimate=pl.CostEstimate(
            flops=4 * rows * heads * 128 * 128, bytes_accessed=2_000_000, transcendentals=0
        ),
        name="suffix",
    )(
        suffix_lengths,
        queries_later,
        suffix_keys.reshape(rows, -1, hdim),
        suffix_values.reshape(rows, -1, hdim),
    )

    attended = pl.pallas_call(
        combine_kernel,
        out_shape=shape((ring, rows, heads * hdim), BF16),
        in_specs=[HBM, HBM, VMEM, HBM],
        out_specs=VMEM,
        scratch_shapes=[
            ints(rows),
            ints(pools),
            pltpu.VMEM((rows, 2 * heads, hdim), F32),
            pltpu.VMEM((pools * (CAP * heads + GROUP), hdim), F32),
            pltpu.VMEM((rows * heads, hdim), F32),
            ints(pools),
            pltpu.SemaphoreType.DMA((3,)),
        ],
        compiler_params=params(8),
        cost_estimate=pl.CostEstimate(flops=0, bytes_accessed=1_000_000, transcendentals=0),
        name="combine",
    )(row_prefix, owner_map, returned, suffix)
    gathered = lax.all_to_all(attended, "y", split_axis=0, concat_axis=0, tiled=True)
    terms = pl.pallas_call(
        project_kernel,
        out_shape=shape((ring, 2, rows, columns), BF16),
        in_specs=[VMEM] * 3,
        out_specs=VMEM,
        compiler_params=params(16),
        cost_estimate=pl.CostEstimate(
            flops=4 * ring * rows * heads * hdim * columns,
            bytes_accessed=4_000_000,
            transcendentals=0,
        ),
        name="project",
    )(gathered, meet(gathered, "core", 1), out_weight)
    shared = lax.all_to_all(
        terms.reshape(lax.axis_size("head"), -1, columns),
        "head",
        split_axis=0,
        concat_axis=0,
        tiled=True,
    )
    return jnp.sum(shared.astype(F32), axis=0).astype(BF16)


def solution(mesh):
    pools, across, groups = mesh.devices.shape
    fine = Mesh(
        mesh.devices.reshape(pools, across // 2, 2, groups), ("pool", "y", "core", "head")
    )
    row = ("y", "core")
    every = ("pool", "y", "core")
    return jax.shard_map(
        body,
        mesh=fine,
        in_specs=(
            P(every, "head", None),
            P("pool", row, "head", None),
            P("pool", row, "head", None),
            P(every, None, "head", None),
            P(every, None, "head", None),
            P(every, None),
            P(),
            P(),
            P(every),
            P("head", row),
        ),
        out_specs=P(("pool", "head"), row),
        check_vma=False,
    )
```

```python
import functools
import math

import jax
import jax.numpy as jnp
from jax import lax
from jax.experimental import pallas as pl
from jax.experimental.pallas import tpu as pltpu
from jax.sharding import Mesh, PartitionSpec as P

LOWEST = -1e30
CAP = 3
GROUP = 8
HD = 128
SCALE = HD**-0.5
LOG2E = math.log2(math.e)
F32 = jnp.float32
BF16 = jnp.bfloat16

VMEM = pl.BlockSpec(memory_space=pltpu.VMEM)
HBM = pl.BlockSpec(memory_space=pltpu.HBM)
TAIL = 16


def params(mib):
    return pltpu.CompilerParams(vmem_limit_bytes=mib * 1024 * 1024)


def split3(value):
    high = value.astype(BF16).astype(F32)
    rest = value - high
    middle = rest.astype(BF16).astype(F32)
    return high, middle, (rest - middle).astype(BF16).astype(F32)


def slot_of(row, row_prefix_ref, owner_ref, count_ref):
    owner = owner_ref[row_prefix_ref[row]]
    place = count_ref[owner]
    count_ref[owner] = place + 1
    return owner, place


def fetch(pairs, sems):
    copies = [pltpu.make_async_copy(*pair, sems.at[i]) for i, pair in enumerate(pairs)]
    for copy in copies:
        copy.start()
    return copies


def dispatch_kernel(
    row_prefix_hbm, owner_hbm, lengths_hbm, q_hbm, k_hbm, v_hbm, out_ref, block_ref,
    row_prefix_ref, owner_ref, lengths_ref, q_ref, mixed, held, count_ref, sems,
):
    copies = fetch(
        (
            (row_prefix_hbm, row_prefix_ref),
            (owner_hbm, owner_ref),
            (lengths_hbm, lengths_ref),
            (q_hbm, q_ref),
            (k_hbm, mixed.at[0]),
            (v_hbm, mixed.at[1]),
        ),
        sems,
    )
    pools = owner_ref.shape[0]
    length = mixed.shape[1] // 2
    for p in range(pools):
        count_ref[p] = 0
    out_ref[...] = jnp.zeros_like(out_ref)
    for copy in copies[:4]:
        copy.wait()
    for r in range(q_ref.shape[0]):
        owner, place = slot_of(r, row_prefix_ref, owner_ref, count_ref)
        out_ref[owner * CAP + place] = q_ref[r]
    pool = lax.axis_index("pool")
    seen = -(lax.axis_index("y") * 2 + lax.axis_index("core")) * length
    for p in range(pools):
        seen += jnp.where(owner_ref[p] == pool, lengths_ref[p], 0)
    tail = (TAIL, HD)
    token = lax.broadcasted_iota(jnp.int32, tail, 0) * HD + lax.broadcasted_iota(jnp.int32, tail, 1)
    block_ref[pl.ds(4 * length, TAIL), :] = jnp.where(token < seen, 0.0, LOWEST).astype(BF16)
    for n in range(2):
        copies[4 + n].wait()
        held[n] = mixed[n].astype(F32)
        for g in range(2):
            block_ref[pl.ds((2 * n + g) * length, length), :] = held[
                n, pl.ds(g, length, stride=2), :
            ].astype(BF16)


def attend_kernel(q_ref, *refs):
    blocks, out_ref = refs[:-1], refs[-1]
    slots = q_ref.shape[0]
    step_slots = math.gcd(24, slots)
    length = (blocks[0].shape[0] - TAIL) // 4
    width = min(512, length)
    units = [(start, g) for start in range(0, slots, step_slots) for g in range(2)]
    pieces = [(block, at) for block in blocks for at in range(0, length, width)]
    lane = lax.broadcasted_iota(jnp.int32, (GROUP, 128), 1)
    ones = jnp.ones((width, HD), BF16)
    tails = [block[pl.ds(4 * length, TAIL), :].astype(F32) for block in blocks]
    biases = [
        jnp.concatenate(
            [tail[row : row + 1] for row in range(at // HD, (at + width) // HD)], axis=1
        )
        for tail in tails
        for at in range(0, length, width)
    ]

    def query(unit):
        start, g = unit
        held = q_ref[pl.ds(start, step_slots)].astype(F32)[:, g * GROUP : (g + 1) * GROUP, :]
        return held.reshape(step_slots * GROUP, HD).astype(BF16)

    def score(q, g, n):
        block, at = pieces[n]
        keys = block[pl.ds(g * length + at, width), :]
        return (
            lax.dot_general(q, keys, (((1,), (1,)), ((), ())), preferred_element_type=F32)
            + biases[n]
        )

    packed = [jnp.zeros((GROUP, 128), F32)] * 2
    kept = {}
    q = query(units[0])
    scores = [score(q, units[0][1], n) for n in range(len(pieces))]
    for i, (start, g) in enumerate(units):
        peak = functools.reduce(
            jnp.maximum, [jnp.max(part, axis=1, keepdims=True) for part in scores]
        )
        peak = jnp.maximum(peak, 0.1 * LOWEST)
        coming = []
        both = None
        if i + 1 < len(units):
            q = query(units[i + 1])
        for n, (block, at) in enumerate(pieces):
            weights = jnp.exp2((scores[n] - peak) * (SCALE * LOG2E)).astype(BF16)
            if i + 1 < len(units):
                coming.append(score(q, units[i + 1][1], n))
            values = jnp.concatenate(
                [block[pl.ds((2 + g) * length + at, width), :], ones], axis=1
            )
            term = jnp.dot(weights, values, preferred_element_type=F32)
            both = term if both is None else both + term
        scores = coming
        total = both[:, HD:]
        live = total > 0
        safe = jnp.where(live, total, 1.0)
        kept[g] = (both[:, :HD] / safe).reshape(step_slots, GROUP, HD)
        lse = jnp.where(live, peak * SCALE + jnp.log(safe), LOWEST)
        lse = lse.reshape(step_slots, GROUP, HD)
        for s in range(step_slots):
            packed[g] = jnp.where(lane == start + s, lse[s], packed[g])
        if g == 1:
            out_ref[pl.ds(start, step_slots)] = jnp.concatenate(
                [kept[0], kept[1]], axis=1
            ).astype(BF16)
    for i, plane in enumerate(split3(jnp.concatenate(packed, axis=0))):
        out_ref[slots + i] = plane.astype(BF16)


def merge_kernel(a_ref, b_ref, c_ref, out_ref):
    blocks = (a_ref, b_ref, c_ref)
    slots = a_ref.shape[0] - 3
    pools = slots // CAP
    lses = [
        (ref[slots + 2].astype(F32) + ref[slots + 1].astype(F32)) + ref[slots].astype(F32)
        for ref in blocks
    ]
    top = functools.reduce(jnp.maximum, lses)
    shares = [jnp.exp(lse - top) for lse in lses]
    total = functools.reduce(jnp.add, shares)
    weights = [share / total for share in shares]
    planes = split3(top + jnp.log(total))
    lane = lax.broadcasted_iota(jnp.int32, (GROUP, 128), 1)
    for pair in range(0, pools, 2):
        rows = []
        for p in (pair, pair + 1):
            for s in range(p * CAP, (p + 1) * CAP):
                terms = [
                    weight[:, s : s + 1] * ref[s].astype(F32) for weight, ref in zip(weights, blocks)
                ]
                rows.append(functools.reduce(jnp.add, terms))
            tile = jnp.zeros((GROUP, 128), F32)
            for i, plane in enumerate(planes):
                for g in range(2):
                    at = i * 16 + g * 8
                    moved = plane[g * GROUP : (g + 1) * GROUP]
                    shift = (at - p * CAP) % 128
                    if shift:
                        moved = pltpu.roll(moved, shift, 1)
                    tile = jnp.where((lane >= at) & (lane < at + CAP), moved, tile)
            rows.append(tile)
        height = CAP * 16 + GROUP
        out_ref[pl.ds(pair * height, 2 * height), :] = jnp.concatenate(rows, axis=0).astype(BF16)


def suffix_kernel(length_hbm, q_ref, k_ref, v_ref, out_ref, length_ref, sems):
    fetch(((length_hbm, length_ref),), sems)[0].wait()
    span = k_ref.shape[1]
    column = lax.broadcasted_iota(jnp.int32, (2 * GROUP, span), 1)
    head = lax.broadcasted_iota(jnp.int32, (2 * GROUP, span), 0)
    same = (column & 1) == head // GROUP
    for r in range(q_ref.shape[0]):
        scores = lax.dot_general(
            q_ref[r], k_ref[r], (((1,), (1,)), ((), ())), preferred_element_type=F32
        )
        visible = same & (column < 2 * length_ref[r])
        scores = jnp.where(visible, scores * SCALE, LOWEST)
        peak = jnp.max(scores, axis=1, keepdims=True)
        powers = jnp.exp(scores - peak)
        total = jnp.sum(powers, axis=1, keepdims=True)
        summed = jnp.dot(powers.astype(BF16), v_ref[r], preferred_element_type=F32)
        out_ref[r, : 2 * GROUP] = summed / total
        out_ref[r, 2 * GROUP :] = jnp.broadcast_to(peak + jnp.log(total), (2 * GROUP, HD))


def combine_kernel(
    row_prefix_hbm, owner_hbm, got_ref, suffix_hbm, out_ref,
    row_prefix_ref, owner_ref, suffix_ref, wide, mixed, count_ref, sems,
):
    copies = fetch(
        (
            (row_prefix_hbm, row_prefix_ref),
            (owner_hbm, owner_ref),
            (suffix_hbm, suffix_ref),
        ),
        sems,
    )
    rows = suffix_ref.shape[0]
    height = CAP * 16 + GROUP
    for p in range(owner_ref.shape[0]):
        count_ref[p] = 0
    wide[...] = got_ref[...].astype(F32)
    for copy in copies:
        copy.wait()
    lane = lax.broadcasted_iota(jnp.int32, (GROUP, 128), 1)
    for r in range(rows):
        owner, place = slot_of(r, row_prefix_ref, owner_ref, count_ref)
        base = owner * height
        prefix = wide[pl.ds(pl.multiple_of(base + place * 16, 8), 16), :]
        tile = wide[pl.ds(pl.multiple_of(base + CAP * 16, 8), GROUP), :]
        lses = []
        for g in range(2):
            chosen = ((lane & 15) == place + g * 8) & (lane < 48)
            lses.append(jnp.sum(jnp.where(chosen, tile, 0.0), axis=1, keepdims=True))
        prefix_lse = jnp.broadcast_to(jnp.concatenate(lses, axis=0), (2 * GROUP, HD))
        suffix_lse = suffix_ref[r, 2 * GROUP :]
        highest = jnp.maximum(prefix_lse, suffix_lse)
        a = jnp.exp(prefix_lse - highest)
        b = jnp.exp(suffix_lse - highest)
        mixed[r * 16 : (r + 1) * 16, :] = (a * prefix + b * suffix_ref[r, : 2 * GROUP]) / (a + b)
    for h in range(2 * GROUP):
        out_ref[:, h * HD : (h + 1) * HD] = mixed[pl.ds(h, rows, stride=16), :].astype(BF16)


def project_kernel(attended_ref, own_ref, other_ref, out_ref):
    core = lax.axis_index("core")
    for at, w_ref in ((core, own_ref), (1 - core, other_ref)):
        out_ref[at] = jnp.dot(
            attended_ref[...], w_ref[...], preferred_element_type=F32
        ).astype(BF16)


def body(
    queries,
    prefix_keys,
    prefix_values,
    suffix_keys,
    suffix_values,
    row_prefix,
    owner_map,
    prefix_lengths,
    suffix_lengths,
    out_weight,
):
    rows, heads, hdim = queries.shape
    row_prefix = row_prefix.reshape(-1)
    pools = lax.axis_size("pool")
    ring = lax.axis_size("y")
    slots = pools * CAP
    columns = out_weight.shape[1]
    shape = jax.ShapeDtypeStruct

    def meet(value, axis, apart):
        pairs = [(i, i ^ apart) for i in range(lax.axis_size(axis))]
        return lax.ppermute(value, axis, pairs)

    def ints(count):
        return pltpu.SMEM((count,), jnp.int32)

    length = prefix_keys.shape[1]
    outgoing, own = pl.pallas_call(
        dispatch_kernel,
        out_shape=[shape((slots, heads, hdim), BF16), shape((4 * length + TAIL, hdim), BF16)],
        in_specs=[HBM] * 6,
        out_specs=[VMEM] * 2,
        scratch_shapes=[
            ints(rows),
            ints(pools),
            ints(pools),
            pltpu.VMEM((rows, heads, hdim), BF16),
            pltpu.VMEM((2, 2 * length, hdim), BF16),
            pltpu.VMEM((2, 2 * length, hdim), F32),
            ints(pools),
            pltpu.SemaphoreType.DMA((6,)),
        ],
        compiler_params=params(60),
        cost_estimate=pl.CostEstimate(flops=0, bytes_accessed=3_000_000, transcendentals=0),
        name="dispatch",
    )(
        row_prefix,
        owner_map,
        prefix_lengths,
        queries,
        prefix_keys.reshape(-1, hdim),
        prefix_values.reshape(-1, hdim),
    )

    arrived = lax.all_to_all(
        outgoing.reshape(pools, CAP, heads, hdim), "pool", split_axis=0, concat_axis=0, tiled=True
    ).reshape(slots, heads, hdim)
    asked = meet(arrived, "y", 1)

    pair, arrived_later = lax.optimization_barrier((meet(own, "y", 3), arrived))
    blocks = {(0, 0): own, (0, 1): meet(own, "core", 1), (1, 0): pair, (1, 1): meet(pair, "core", 1)}

    def attend(q, *sources):
        span = len(sources) * length
        return pl.pallas_call(
            attend_kernel,
            out_shape=shape((slots + 3, heads, hdim), BF16),
            in_specs=[VMEM] * (1 + len(sources)),
            out_specs=VMEM,
            compiler_params=params(30),
            cost_estimate=pl.CostEstimate(
                flops=6 * slots * heads * span * hdim,
                bytes_accessed=3_000_000,
                transcendentals=slots * heads * span,
            ),
            name="attend",
        )(q, *(blocks[source] for source in sources))

    near, far = ((0, 0), (0, 1)), ((1, 0), (1, 1))
    near_part, asked = lax.optimization_barrier((attend(arrived, *near), asked))
    answer = meet(attend(asked, *near, *far), "y", 1)
    far_part = attend(arrived_later, *far)
    merged = pl.pallas_call(
        merge_kernel,
        out_shape=shape((pools * (CAP * heads + GROUP), hdim), BF16),
        in_specs=[VMEM] * 3,
        out_specs=VMEM,
        compiler_params=params(8),
        cost_estimate=pl.CostEstimate(flops=0, bytes_accessed=1_000_000, transcendentals=0),
        name="merge",
    )(near_part, far_part, answer)
    merged, queries_later, weight = lax.optimization_barrier((merged, queries, out_weight))
    other_weight = meet(weight, "core", 1)
    returned = lax.all_to_all(
        merged.reshape(pools, CAP * heads + GROUP, hdim),
        "pool",
        split_axis=0,
        concat_axis=0,
        tiled=True,
    ).reshape(-1, hdim)

    returned, other_weight = lax.optimization_barrier((returned, other_weight))
    suffix = pl.pallas_call(
        suffix_kernel,
        out_shape=shape((rows, 2 * heads, hdim), F32),
        in_specs=[HBM, VMEM, VMEM, VMEM],
        out_specs=VMEM,
        scratch_shapes=[ints(rows), pltpu.SemaphoreType.DMA((1,))],
        compiler_params=params(8),
        cost_estimate=pl.CostEstimate(
            flops=4 * rows * heads * 128 * 128, bytes_accessed=2_000_000, transcendentals=0
        ),
        name="suffix",
    )(
        suffix_lengths,
        queries_later,
        suffix_keys.reshape(rows, -1, hdim),
        suffix_values.reshape(rows, -1, hdim),
    )

    attended = pl.pallas_call(
        combine_kernel,
        out_shape=shape((rows, heads * hdim), BF16),
        in_specs=[HBM, HBM, VMEM, HBM],
        out_specs=VMEM,
        scratch_shapes=[
            ints(rows),
            ints(pools),
            pltpu.VMEM((rows, 2 * heads, hdim), F32),
            pltpu.VMEM((pools * (CAP * heads + GROUP), hdim), F32),
            pltpu.VMEM((rows * heads, hdim), F32),
            ints(pools),
            pltpu.SemaphoreType.DMA((3,)),
        ],
        compiler_params=params(8),
        cost_estimate=pl.CostEstimate(flops=0, bytes_accessed=1_000_000, transcendentals=0),
        name="combine",
    )(row_prefix, owner_map, returned, suffix)
    gathered = lax.all_gather(attended, "y", axis=0, tiled=True)
    terms = pl.pallas_call(
        project_kernel,
        out_shape=shape((2, ring * rows, columns), BF16),
        in_specs=[VMEM] * 3,
        out_specs=VMEM,
        compiler_params=params(16),
        cost_estimate=pl.CostEstimate(
            flops=4 * ring * rows * heads * hdim * columns,
            bytes_accessed=6_000_000,
            transcendentals=0,
        ),
        name="project",
    )(gathered, out_weight, other_weight)
    groups = lax.axis_size("head")
    shared = lax.all_to_all(
        terms.reshape(2 * groups, -1, columns),
        ("core", "head"),
        split_axis=0,
        concat_axis=0,
        tiled=True,
    )
    shared = shared.reshape(2, groups, -1, columns).astype(F32)
    return jnp.sum(shared, axis=1).astype(BF16).reshape(-1, columns)


def solution(mesh):
    pools, across, groups = mesh.devices.shape
    fine = Mesh(
        mesh.devices.reshape(pools, across // 2, 2, groups), ("pool", "y", "core", "head")
    )
    row = ("y", "core")
    every = ("pool", "y", "core")
    return jax.shard_map(
        body,
        mesh=fine,
        in_specs=(
            P(every, "head", None),
            P("pool", row, "head", None),
            P("pool", row, "head", None),
            P(every, None, "head", None),
            P(every, None, "head", None),
            P(every, None),
            P(),
            P(),
            P(every),
            P("head", row),
        ),
        out_specs=P(("pool", "head"), row),
        check_vma=False,
    )
```

```python
import functools
import math

import jax
import jax.numpy as jnp
from jax import lax
from jax.experimental import pallas as pl
from jax.experimental.pallas import tpu as pltpu
from jax.sharding import Mesh, PartitionSpec as P

LOWEST = -1e30
CAP = 3
GROUP = 8
HD = 128
SCALE = HD**-0.5
LOG2E = math.log2(math.e)
F32 = jnp.float32
BF16 = jnp.bfloat16

VMEM = pl.BlockSpec(memory_space=pltpu.VMEM)
HBM = pl.BlockSpec(memory_space=pltpu.HBM)
TAIL = 16


def params(mib):
    return pltpu.CompilerParams(vmem_limit_bytes=mib * 1024 * 1024)


def split3(value):
    high = value.astype(BF16).astype(F32)
    rest = value - high
    middle = rest.astype(BF16).astype(F32)
    return high, middle, (rest - middle).astype(BF16).astype(F32)


def slot_of(row, row_prefix_ref, owner_ref, count_ref):
    owner = owner_ref[row_prefix_ref[row]]
    place = count_ref[owner]
    count_ref[owner] = place + 1
    return owner, place


def fetch(pairs, sems):
    copies = [pltpu.make_async_copy(*pair, sems.at[i]) for i, pair in enumerate(pairs)]
    for copy in copies:
        copy.start()
    return copies


def dispatch_kernel(
    row_prefix_hbm, owner_hbm, lengths_hbm, q_hbm, k_hbm, v_hbm, out_ref, block_ref,
    row_prefix_ref, owner_ref, lengths_ref, q_ref, mixed, held, count_ref, sems,
):
    copies = fetch(
        (
            (row_prefix_hbm, row_prefix_ref),
            (owner_hbm, owner_ref),
            (lengths_hbm, lengths_ref),
            (q_hbm, q_ref),
            (k_hbm, mixed.at[0]),
            (v_hbm, mixed.at[1]),
        ),
        sems,
    )
    pools = owner_ref.shape[0]
    length = mixed.shape[1] // 2
    for p in range(pools):
        count_ref[p] = 0
    out_ref[...] = jnp.zeros_like(out_ref)
    for copy in copies[:4]:
        copy.wait()
    for r in range(q_ref.shape[0]):
        owner, place = slot_of(r, row_prefix_ref, owner_ref, count_ref)
        out_ref[owner * CAP + place] = q_ref[r]
    pool = lax.axis_index("pool")
    seen = -(lax.axis_index("y") * 2 + lax.axis_index("core")) * length
    for p in range(pools):
        seen += jnp.where(owner_ref[p] == pool, lengths_ref[p], 0)
    tail = (TAIL, HD)
    token = lax.broadcasted_iota(jnp.int32, tail, 0) * HD + lax.broadcasted_iota(jnp.int32, tail, 1)
    block_ref[pl.ds(4 * length, TAIL), :] = jnp.where(token < seen, 0.0, LOWEST).astype(BF16)
    for n in range(2):
        copies[4 + n].wait()
        held[n] = mixed[n].astype(F32)
        for g in range(2):
            block_ref[pl.ds((2 * n + g) * length, length), :] = held[
                n, pl.ds(g, length, stride=2), :
            ].astype(BF16)


def unpack_lse(ref):
    slots = ref.shape[0] - 3
    high, middle, low = (ref[slots + i].astype(F32) for i in range(3))
    return (low + middle) + high


def attend_kernel(merging, q_ref, *refs):
    earlier_ref = refs[0] if merging else None
    blocks, out_ref = refs[int(merging) : -1], refs[-1]
    slots = q_ref.shape[0]
    step_slots = math.gcd(24, slots)
    length = (blocks[0].shape[0] - TAIL) // 4
    width = min(512, length)
    units = [(start, g) for start in range(0, slots, step_slots) for g in range(2)]
    pieces = [(block, at) for block in blocks for at in range(0, length, width)]
    lane = lax.broadcasted_iota(jnp.int32, (GROUP, 128), 1)
    ones = jnp.ones((width, HD), BF16)
    tails = [block[pl.ds(4 * length, TAIL), :].astype(F32) for block in blocks]
    biases = [
        jnp.concatenate(
            [tail[row : row + 1] for row in range(at // HD, (at + width) // HD)], axis=1
        )
        for tail in tails
        for at in range(0, length, width)
    ]

    def query(unit):
        start, g = unit
        held = q_ref[pl.ds(start, step_slots)].astype(F32)[:, g * GROUP : (g + 1) * GROUP, :]
        return held.reshape(step_slots * GROUP, HD).astype(BF16)

    def score(q, g, n):
        block, at = pieces[n]
        keys = block[pl.ds(g * length + at, width), :]
        return (
            lax.dot_general(q, keys, (((1,), (1,)), ((), ())), preferred_element_type=F32)
            + biases[n]
        )

    if merging:
        earlier_lse = unpack_lse(earlier_ref)
    packed = [jnp.zeros((GROUP, 128), F32)] * 2
    kept = {}
    q = query(units[0])
    scores = [score(q, units[0][1], n) for n in range(len(pieces))]
    for i, (start, g) in enumerate(units):
        peak = functools.reduce(
            jnp.maximum, [jnp.max(part, axis=1, keepdims=True) for part in scores]
        )
        peak = jnp.maximum(peak, 0.1 * LOWEST)
        coming = []
        both = None
        if i + 1 < len(units):
            q = query(units[i + 1])
        for n, (block, at) in enumerate(pieces):
            weights = jnp.exp2((scores[n] - peak) * (SCALE * LOG2E)).astype(BF16)
            if i + 1 < len(units):
                coming.append(score(q, units[i + 1][1], n))
            values = jnp.concatenate(
                [block[pl.ds((2 + g) * length + at, width), :], ones], axis=1
            )
            term = jnp.dot(weights, values, preferred_element_type=F32)
            both = term if both is None else both + term
        scores = coming
        total = both[:, HD:]
        live = total > 0
        safe = jnp.where(live, total, 1.0)
        kept[g] = (both[:, :HD] / safe).reshape(step_slots, GROUP, HD)
        lse = jnp.where(live, peak * SCALE + jnp.log(safe), LOWEST)
        lse = lse.reshape(step_slots, GROUP, HD)
        if merging:
            half = slice(g * GROUP, (g + 1) * GROUP)
            before = jnp.stack(
                [
                    jnp.broadcast_to(earlier_lse[half, s : s + 1], (GROUP, HD))
                    for s in range(start, start + step_slots)
                ]
            )
            result = earlier_ref[pl.ds(start, step_slots)].astype(F32)[:, half, :]
            top = jnp.maximum(lse, before)
            a = jnp.exp(lse - top)
            b = jnp.exp(before - top)
            kept[g] = (a * kept[g] + b * result) / (a + b)
            lse = top + jnp.log(a + b)
        for s in range(step_slots):
            packed[g] = jnp.where(lane == start + s, lse[s], packed[g])
        if g == 1:
            out_ref[pl.ds(start, step_slots)] = jnp.concatenate(
                [kept[0], kept[1]], axis=1
            ).astype(BF16)
    for i, plane in enumerate(split3(jnp.concatenate(packed, axis=0))):
        out_ref[slots + i] = plane.astype(BF16)


def merge_kernel(a_ref, b_ref, out_ref):
    blocks = (a_ref, b_ref)
    slots = a_ref.shape[0] - 3
    pools = slots // CAP
    lses = [unpack_lse(ref) for ref in blocks]
    top = functools.reduce(jnp.maximum, lses)
    shares = [jnp.exp(lse - top) for lse in lses]
    total = functools.reduce(jnp.add, shares)
    weights = [share / total for share in shares]
    planes = split3(top + jnp.log(total))
    lane = lax.broadcasted_iota(jnp.int32, (GROUP, 128), 1)
    for pair in range(0, pools, 2):
        rows = []
        for p in (pair, pair + 1):
            for s in range(p * CAP, (p + 1) * CAP):
                terms = [
                    weight[:, s : s + 1] * ref[s].astype(F32) for weight, ref in zip(weights, blocks)
                ]
                rows.append(functools.reduce(jnp.add, terms))
            tile = jnp.zeros((GROUP, 128), F32)
            for i, plane in enumerate(planes):
                for g in range(2):
                    at = i * 16 + g * 8
                    moved = plane[g * GROUP : (g + 1) * GROUP]
                    shift = (at - p * CAP) % 128
                    if shift:
                        moved = pltpu.roll(moved, shift, 1)
                    tile = jnp.where((lane >= at) & (lane < at + CAP), moved, tile)
            rows.append(tile)
        height = CAP * 16 + GROUP
        out_ref[pl.ds(pair * height, 2 * height), :] = jnp.concatenate(rows, axis=0).astype(BF16)


def suffix_kernel(length_hbm, q_ref, k_ref, v_ref, out_ref, length_ref, sems):
    fetch(((length_hbm, length_ref),), sems)[0].wait()
    span = k_ref.shape[1]
    column = lax.broadcasted_iota(jnp.int32, (2 * GROUP, span), 1)
    head = lax.broadcasted_iota(jnp.int32, (2 * GROUP, span), 0)
    same = (column & 1) == head // GROUP
    for r in range(q_ref.shape[0]):
        scores = lax.dot_general(
            q_ref[r], k_ref[r], (((1,), (1,)), ((), ())), preferred_element_type=F32
        )
        visible = same & (column < 2 * length_ref[r])
        scores = jnp.where(visible, scores * SCALE, LOWEST)
        peak = jnp.max(scores, axis=1, keepdims=True)
        powers = jnp.exp(scores - peak)
        total = jnp.sum(powers, axis=1, keepdims=True)
        summed = jnp.dot(powers.astype(BF16), v_ref[r], preferred_element_type=F32)
        out_ref[r, : 2 * GROUP] = summed / total
        out_ref[r, 2 * GROUP :] = jnp.broadcast_to(peak + jnp.log(total), (2 * GROUP, HD))


def combine_kernel(
    row_prefix_hbm, owner_hbm, got_ref, suffix_hbm, out_ref,
    row_prefix_ref, owner_ref, suffix_ref, wide, mixed, count_ref, sems,
):
    copies = fetch(
        (
            (row_prefix_hbm, row_prefix_ref),
            (owner_hbm, owner_ref),
            (suffix_hbm, suffix_ref),
        ),
        sems,
    )
    rows = suffix_ref.shape[0]
    height = CAP * 16 + GROUP
    for p in range(owner_ref.shape[0]):
        count_ref[p] = 0
    wide[...] = got_ref[...].astype(F32)
    for copy in copies:
        copy.wait()
    lane = lax.broadcasted_iota(jnp.int32, (GROUP, 128), 1)
    for r in range(rows):
        owner, place = slot_of(r, row_prefix_ref, owner_ref, count_ref)
        base = owner * height
        prefix = wide[pl.ds(pl.multiple_of(base + place * 16, 8), 16), :]
        tile = wide[pl.ds(pl.multiple_of(base + CAP * 16, 8), GROUP), :]
        lses = []
        for g in range(2):
            chosen = ((lane & 15) == place + g * 8) & (lane < 48)
            lses.append(jnp.sum(jnp.where(chosen, tile, 0.0), axis=1, keepdims=True))
        prefix_lse = jnp.broadcast_to(jnp.concatenate(lses, axis=0), (2 * GROUP, HD))
        suffix_lse = suffix_ref[r, 2 * GROUP :]
        highest = jnp.maximum(prefix_lse, suffix_lse)
        a = jnp.exp(prefix_lse - highest)
        b = jnp.exp(suffix_lse - highest)
        mixed[r * 16 : (r + 1) * 16, :] = (a * prefix + b * suffix_ref[r, : 2 * GROUP]) / (a + b)
    for h in range(2 * GROUP):
        piece = mixed[pl.ds(h, rows, stride=16), :].astype(BF16)
        for n in range(out_ref.shape[0]):
            out_ref[n, :, h * HD : (h + 1) * HD] = piece


def project_kernel(own_ref, other_ref, w_ref, out_ref):
    count, rows, depth = own_ref.shape
    core = lax.axis_index("core")
    both = jnp.concatenate(
        [own_ref[...].reshape(count * rows, depth), other_ref[...].reshape(count * rows, depth)],
        axis=0,
    )
    terms = jnp.dot(both, w_ref[...], preferred_element_type=F32).astype(BF16)
    terms = terms.reshape(2, count, rows, -1)
    for n in range(count):
        out_ref[n, core] = terms[0, n]
        out_ref[n, 1 - core] = terms[1, n]


def body(
    queries,
    prefix_keys,
    prefix_values,
    suffix_keys,
    suffix_values,
    row_prefix,
    owner_map,
    prefix_lengths,
    suffix_lengths,
    out_weight,
):
    rows, heads, hdim = queries.shape
    row_prefix = row_prefix.reshape(-1)
    pools = lax.axis_size("pool")
    ring = lax.axis_size("y")
    slots = pools * CAP
    columns = out_weight.shape[1]
    shape = jax.ShapeDtypeStruct

    def meet(value, axis, apart):
        pairs = [(i, i ^ apart) for i in range(lax.axis_size(axis))]
        return lax.ppermute(value, axis, pairs)

    def ints(count):
        return pltpu.SMEM((count,), jnp.int32)

    length = prefix_keys.shape[1]
    outgoing, own = pl.pallas_call(
        dispatch_kernel,
        out_shape=[shape((slots, heads, hdim), BF16), shape((4 * length + TAIL, hdim), BF16)],
        in_specs=[HBM] * 6,
        out_specs=[VMEM] * 2,
        scratch_shapes=[
            ints(rows),
            ints(pools),
            ints(pools),
            pltpu.VMEM((rows, heads, hdim), BF16),
            pltpu.VMEM((2, 2 * length, hdim), BF16),
            pltpu.VMEM((2, 2 * length, hdim), F32),
            ints(pools),
            pltpu.SemaphoreType.DMA((6,)),
        ],
        compiler_params=params(60),
        cost_estimate=pl.CostEstimate(flops=0, bytes_accessed=3_000_000, transcendentals=0),
        name="dispatch",
    )(
        row_prefix,
        owner_map,
        prefix_lengths,
        queries,
        prefix_keys.reshape(-1, hdim),
        prefix_values.reshape(-1, hdim),
    )

    arrived = lax.all_to_all(
        outgoing.reshape(pools, CAP, heads, hdim), "pool", split_axis=0, concat_axis=0, tiled=True
    ).reshape(slots, heads, hdim)
    asked = meet(arrived, "y", 1)

    pair, arrived_later = lax.optimization_barrier((meet(own, "y", 3), arrived))
    blocks = {(0, 0): own, (0, 1): meet(own, "core", 1), (1, 0): pair}

    def attend(q, sources, earlier=None, times=1):
        span = len(sources) * length
        merging = earlier is not None
        return pl.pallas_call(
            functools.partial(attend_kernel, merging),
            out_shape=shape((slots + 3, heads, hdim), BF16),
            in_specs=[VMEM] * (1 + merging + len(sources)),
            out_specs=VMEM,
            compiler_params=params(30),
            cost_estimate=pl.CostEstimate(
                flops=6 * times * slots * heads * span * hdim,
                bytes_accessed=3_000_000,
                transcendentals=slots * heads * span,
            ),
            name="attend",
        )(q, *([earlier] if merging else []), *(blocks[source] for source in sources))

    near, far = ((0, 0), (0, 1)), ((1, 0), (1, 1))
    first = attend(arrived_later, near[:1])
    blocks[1, 0], first = lax.optimization_barrier((pair, first))
    blocks[1, 1] = meet(blocks[1, 0], "core", 1)
    answer = meet(attend(asked, far, attend(asked, near, times=10)), "y", 1)
    own_part = attend(arrived_later, near[1:] + far, first)
    merged = pl.pallas_call(
        merge_kernel,
        out_shape=shape((pools * (CAP * heads + GROUP), hdim), BF16),
        in_specs=[VMEM] * 2,
        out_specs=VMEM,
        compiler_params=params(8),
        cost_estimate=pl.CostEstimate(flops=0, bytes_accessed=1_000_000, transcendentals=0),
        name="merge",
    )(own_part, answer)
    merged, queries_later = lax.optimization_barrier((merged, queries))
    returned = lax.all_to_all(
        merged.reshape(pools, CAP * heads + GROUP, hdim),
        "pool",
        split_axis=0,
        concat_axis=0,
        tiled=True,
    ).reshape(-1, hdim)

    suffix = pl.pallas_call(
        suffix_kernel,
        out_shape=shape((rows, 2 * heads, hdim), F32),
        in_specs=[HBM, VMEM, VMEM, VMEM],
        out_specs=VMEM,
        scratch_shapes=[ints(rows), pltpu.SemaphoreType.DMA((1,))],
        compiler_params=params(8),
        cost_estimate=pl.CostEstimate(
            flops=4 * rows * heads * 128 * 128, bytes_accessed=2_000_000, transcendentals=0
        ),
        name="suffix",
    )(
        suffix_lengths,
        queries_later,
        suffix_keys.reshape(rows, -1, hdim),
        suffix_values.reshape(rows, -1, hdim),
    )

    attended = pl.pallas_call(
        combine_kernel,
        out_shape=shape((ring, rows, heads * hdim), BF16),
        in_specs=[HBM, HBM, VMEM, HBM],
        out_specs=VMEM,
        scratch_shapes=[
            ints(rows),
            ints(pools),
            pltpu.VMEM((rows, 2 * heads, hdim), F32),
            pltpu.VMEM((pools * (CAP * heads + GROUP), hdim), F32),
            pltpu.VMEM((rows * heads, hdim), F32),
            ints(pools),
            pltpu.SemaphoreType.DMA((3,)),
        ],
        compiler_params=params(8),
        cost_estimate=pl.CostEstimate(flops=0, bytes_accessed=1_000_000, transcendentals=0),
        name="combine",
    )(row_prefix, owner_map, returned, suffix)
    gathered = lax.all_to_all(attended, "y", split_axis=0, concat_axis=0, tiled=True)
    terms = pl.pallas_call(
        project_kernel,
        out_shape=shape((ring, 2, rows, columns), BF16),
        in_specs=[VMEM] * 3,
        out_specs=VMEM,
        compiler_params=params(16),
        cost_estimate=pl.CostEstimate(
            flops=4 * ring * rows * heads * hdim * columns,
            bytes_accessed=4_000_000,
            transcendentals=0,
        ),
        name="project",
    )(gathered, meet(gathered, "core", 1), out_weight)
    shared = lax.all_to_all(
        terms.reshape(lax.axis_size("head"), -1, columns),
        "head",
        split_axis=0,
        concat_axis=0,
        tiled=True,
    )
    return jnp.sum(shared.astype(F32), axis=0).astype(BF16)


def solution(mesh):
    pools, across, groups = mesh.devices.shape
    fine = Mesh(
        mesh.devices.reshape(pools, across // 2, 2, groups), ("pool", "y", "core", "head")
    )
    row = ("y", "core")
    every = ("pool", "y", "core")
    return jax.shard_map(
        body,
        mesh=fine,
        in_specs=(
            P(every, "head", None),
            P("pool", row, "head", None),
            P("pool", row, "head", None),
            P(every, None, "head", None),
            P(every, None, "head", None),
            P(every, None),
            P(),
            P(),
            P(every),
            P("head", row),
        ),
        out_specs=P(("pool", "head"), row),
        check_vma=False,
    )
```

```python
import functools
import math

import jax
import jax.numpy as jnp
from jax import lax
from jax.experimental import pallas as pl
from jax.experimental.pallas import tpu as pltpu
from jax.sharding import Mesh, PartitionSpec as P

LOWEST = -1e30
CAP = 3
GROUP = 8
HD = 128
SCALE = HD**-0.5
LOG2E = math.log2(math.e)
F32 = jnp.float32
BF16 = jnp.bfloat16

VMEM = pl.BlockSpec(memory_space=pltpu.VMEM)
HBM = pl.BlockSpec(memory_space=pltpu.HBM)
TAIL = 16


def params(mib):
    return pltpu.CompilerParams(vmem_limit_bytes=mib * 1024 * 1024)


def split3(value):
    high = value.astype(BF16).astype(F32)
    rest = value - high
    middle = rest.astype(BF16).astype(F32)
    return high, middle, (rest - middle).astype(BF16).astype(F32)


def slot_of(row, row_prefix_ref, owner_ref, count_ref):
    owner = owner_ref[row_prefix_ref[row]]
    place = count_ref[owner]
    count_ref[owner] = place + 1
    return owner, place


def fetch(pairs, sems):
    copies = [pltpu.make_async_copy(*pair, sems.at[i]) for i, pair in enumerate(pairs)]
    for copy in copies:
        copy.start()
    return copies


def dispatch_kernel(
    row_prefix_hbm, owner_hbm, lengths_hbm, q_hbm, k_hbm, v_hbm, out_ref, block_ref,
    row_prefix_ref, owner_ref, lengths_ref, q_ref, mixed, held, count_ref, sems,
):
    copies = fetch(
        (
            (row_prefix_hbm, row_prefix_ref),
            (owner_hbm, owner_ref),
            (lengths_hbm, lengths_ref),
            (q_hbm, q_ref),
            (k_hbm, mixed.at[0]),
            (v_hbm, mixed.at[1]),
        ),
        sems,
    )
    pools = owner_ref.shape[0]
    length = mixed.shape[1] // 2
    for p in range(pools):
        count_ref[p] = 0
    out_ref[...] = jnp.zeros_like(out_ref)
    for copy in copies[:4]:
        copy.wait()
    for r in range(q_ref.shape[0]):
        owner, place = slot_of(r, row_prefix_ref, owner_ref, count_ref)
        out_ref[owner * CAP + place] = q_ref[r]
    pool = lax.axis_index("pool")
    seen = -(lax.axis_index("y") * 2 + lax.axis_index("core")) * length
    for p in range(pools):
        seen += jnp.where(owner_ref[p] == pool, lengths_ref[p], 0)
    tail = (TAIL, HD)
    token = lax.broadcasted_iota(jnp.int32, tail, 0) * HD + lax.broadcasted_iota(jnp.int32, tail, 1)
    block_ref[pl.ds(4 * length, TAIL), :] = jnp.where(token < seen, 0.0, LOWEST).astype(BF16)
    for n in range(2):
        copies[4 + n].wait()
        held[n] = mixed[n].astype(F32)
        for g in range(2):
            block_ref[pl.ds((2 * n + g) * length, length), :] = held[
                n, pl.ds(g, length, stride=2), :
            ].astype(BF16)


def unpack_lse(ref):
    slots = ref.shape[0] - 3
    high, middle, low = (ref[slots + i].astype(F32) for i in range(3))
    return (low + middle) + high


def attend_kernel(merging, q_ref, *refs):
    earlier_ref = refs[0] if merging else None
    blocks, out_ref = refs[int(merging) : -1], refs[-1]
    slots = q_ref.shape[0]
    step_slots = math.gcd(24, slots)
    length = (blocks[0].shape[0] - TAIL) // 4
    width = min(512, length)
    units = [(start, g) for start in range(0, slots, step_slots) for g in range(2)]
    pieces = [(block, at) for block in blocks for at in range(0, length, width)]
    lane = lax.broadcasted_iota(jnp.int32, (GROUP, 128), 1)
    ones = jnp.ones((width, HD), BF16)
    tails = [block[pl.ds(4 * length, TAIL), :].astype(F32) for block in blocks]
    biases = [
        jnp.concatenate(
            [tail[row : row + 1] for row in range(at // HD, (at + width) // HD)], axis=1
        )
        for tail in tails
        for at in range(0, length, width)
    ]

    def query(unit):
        start, g = unit
        held = q_ref[pl.ds(start, step_slots)].astype(F32)[:, g * GROUP : (g + 1) * GROUP, :]
        return held.reshape(step_slots * GROUP, HD).astype(BF16)

    def score(q, g, n):
        block, at = pieces[n]
        keys = block[pl.ds(g * length + at, width), :]
        return (
            lax.dot_general(q, keys, (((1,), (1,)), ((), ())), preferred_element_type=F32)
            + biases[n]
        )

    if merging:
        earlier_lse = unpack_lse(earlier_ref)
    packed = [jnp.zeros((GROUP, 128), F32)] * 2
    kept = {}
    q = query(units[0])
    scores = [score(q, units[0][1], n) for n in range(len(pieces))]
    for i, (start, g) in enumerate(units):
        peak = functools.reduce(
            jnp.maximum, [jnp.max(part, axis=1, keepdims=True) for part in scores]
        )
        peak = jnp.maximum(peak, 0.1 * LOWEST)
        coming = []
        both = None
        if i + 1 < len(units):
            q = query(units[i + 1])
        for n, (block, at) in enumerate(pieces):
            weights = jnp.exp2((scores[n] - peak) * (SCALE * LOG2E)).astype(BF16)
            if i + 1 < len(units):
                coming.append(score(q, units[i + 1][1], n))
            values = jnp.concatenate(
                [block[pl.ds((2 + g) * length + at, width), :], ones], axis=1
            )
            term = jnp.dot(weights, values, preferred_element_type=F32)
            both = term if both is None else both + term
        scores = coming
        total = both[:, HD:]
        live = total > 0
        safe = jnp.where(live, total, 1.0)
        kept[g] = (both[:, :HD] / safe).reshape(step_slots, GROUP, HD)
        lse = jnp.where(live, peak * SCALE + jnp.log(safe), LOWEST)
        lse = lse.reshape(step_slots, GROUP, HD)
        if merging:
            half = slice(g * GROUP, (g + 1) * GROUP)
            before = jnp.stack(
                [
                    jnp.broadcast_to(earlier_lse[half, s : s + 1], (GROUP, HD))
                    for s in range(start, start + step_slots)
                ]
            )
            result = earlier_ref[pl.ds(start, step_slots)].astype(F32)[:, half, :]
            top = jnp.maximum(lse, before)
            a = jnp.exp(lse - top)
            b = jnp.exp(before - top)
            kept[g] = (a * kept[g] + b * result) / (a + b)
            lse = top + jnp.log(a + b)
        for s in range(step_slots):
            packed[g] = jnp.where(lane == start + s, lse[s], packed[g])
        if g == 1:
            out_ref[pl.ds(start, step_slots)] = jnp.concatenate(
                [kept[0], kept[1]], axis=1
            ).astype(BF16)
    for i, plane in enumerate(split3(jnp.concatenate(packed, axis=0))):
        out_ref[slots + i] = plane.astype(BF16)


def merge_kernel(a_ref, b_ref, out_ref):
    blocks = (a_ref, b_ref)
    slots = a_ref.shape[0] - 3
    pools = slots // CAP
    lses = [unpack_lse(ref) for ref in blocks]
    top = functools.reduce(jnp.maximum, lses)
    shares = [jnp.exp(lse - top) for lse in lses]
    total = functools.reduce(jnp.add, shares)
    weights = [share / total for share in shares]
    planes = split3(top + jnp.log(total))
    lane = lax.broadcasted_iota(jnp.int32, (GROUP, 128), 1)
    for pair in range(0, pools, 2):
        rows = []
        for p in (pair, pair + 1):
            for s in range(p * CAP, (p + 1) * CAP):
                terms = [
                    weight[:, s : s + 1] * ref[s].astype(F32) for weight, ref in zip(weights, blocks)
                ]
                rows.append(functools.reduce(jnp.add, terms))
            tile = jnp.zeros((GROUP, 128), F32)
            for i, plane in enumerate(planes):
                for g in range(2):
                    at = i * 16 + g * 8
                    moved = plane[g * GROUP : (g + 1) * GROUP]
                    shift = (at - p * CAP) % 128
                    if shift:
                        moved = pltpu.roll(moved, shift, 1)
                    tile = jnp.where((lane >= at) & (lane < at + CAP), moved, tile)
            rows.append(tile)
        height = CAP * 16 + GROUP
        out_ref[pl.ds(pair * height, 2 * height), :] = jnp.concatenate(rows, axis=0).astype(BF16)


def suffix_kernel(length_hbm, q_ref, k_ref, v_ref, out_ref, length_ref, sems):
    fetch(((length_hbm, length_ref),), sems)[0].wait()
    span = k_ref.shape[1]
    column = lax.broadcasted_iota(jnp.int32, (2 * GROUP, span), 1)
    head = lax.broadcasted_iota(jnp.int32, (2 * GROUP, span), 0)
    same = (column & 1) == head // GROUP
    for r in range(q_ref.shape[0]):
        scores = lax.dot_general(
            q_ref[r], k_ref[r], (((1,), (1,)), ((), ())), preferred_element_type=F32
        )
        visible = same & (column < 2 * length_ref[r])
        scores = jnp.where(visible, scores * SCALE, LOWEST)
        peak = jnp.max(scores, axis=1, keepdims=True)
        powers = jnp.exp(scores - peak)
        total = jnp.sum(powers, axis=1, keepdims=True)
        summed = jnp.dot(powers.astype(BF16), v_ref[r], preferred_element_type=F32)
        out_ref[r, : 2 * GROUP] = summed / total
        out_ref[r, 2 * GROUP :] = jnp.broadcast_to(peak + jnp.log(total), (2 * GROUP, HD))


def combine_kernel(
    row_prefix_hbm, owner_hbm, got_ref, suffix_hbm, out_ref,
    row_prefix_ref, owner_ref, suffix_ref, wide, mixed, count_ref, sems,
):
    copies = fetch(
        (
            (row_prefix_hbm, row_prefix_ref),
            (owner_hbm, owner_ref),
            (suffix_hbm, suffix_ref),
        ),
        sems,
    )
    rows = suffix_ref.shape[0]
    height = CAP * 16 + GROUP
    for p in range(owner_ref.shape[0]):
        count_ref[p] = 0
    wide[...] = got_ref[...].astype(F32)
    for copy in copies:
        copy.wait()
    lane = lax.broadcasted_iota(jnp.int32, (GROUP, 128), 1)
    for r in range(rows):
        owner, place = slot_of(r, row_prefix_ref, owner_ref, count_ref)
        base = owner * height
        prefix = wide[pl.ds(pl.multiple_of(base + place * 16, 8), 16), :]
        tile = wide[pl.ds(pl.multiple_of(base + CAP * 16, 8), GROUP), :]
        lses = []
        for g in range(2):
            chosen = ((lane & 15) == place + g * 8) & (lane < 48)
            lses.append(jnp.sum(jnp.where(chosen, tile, 0.0), axis=1, keepdims=True))
        prefix_lse = jnp.broadcast_to(jnp.concatenate(lses, axis=0), (2 * GROUP, HD))
        suffix_lse = suffix_ref[r, 2 * GROUP :]
        highest = jnp.maximum(prefix_lse, suffix_lse)
        a = jnp.exp(prefix_lse - highest)
        b = jnp.exp(suffix_lse - highest)
        mixed[r * 16 : (r + 1) * 16, :] = (a * prefix + b * suffix_ref[r, : 2 * GROUP]) / (a + b)
    for h in range(2 * GROUP):
        piece = mixed[pl.ds(h, rows, stride=16), :].astype(BF16)
        for n in range(out_ref.shape[0]):
            out_ref[n, :, h * HD : (h + 1) * HD] = piece


def project_kernel(own_ref, other_ref, w_ref, out_ref):
    count, rows, depth = own_ref.shape
    core = lax.axis_index("core")
    both = jnp.concatenate(
        [own_ref[...].reshape(count * rows, depth), other_ref[...].reshape(count * rows, depth)],
        axis=0,
    )
    terms = jnp.dot(both, w_ref[...], preferred_element_type=F32).astype(BF16)
    terms = terms.reshape(2, count, rows, -1)
    for n in range(count):
        out_ref[n, core] = terms[0, n]
        out_ref[n, 1 - core] = terms[1, n]


def body(
    queries,
    prefix_keys,
    prefix_values,
    suffix_keys,
    suffix_values,
    row_prefix,
    owner_map,
    prefix_lengths,
    suffix_lengths,
    out_weight,
):
    rows, heads, hdim = queries.shape
    row_prefix = row_prefix.reshape(-1)
    pools = lax.axis_size("pool")
    ring = lax.axis_size("y")
    slots = pools * CAP
    columns = out_weight.shape[1]
    shape = jax.ShapeDtypeStruct

    def meet(value, axis, apart):
        pairs = [(i, i ^ apart) for i in range(lax.axis_size(axis))]
        return lax.ppermute(value, axis, pairs)

    def ints(count):
        return pltpu.SMEM((count,), jnp.int32)

    length = prefix_keys.shape[1]
    outgoing, own = pl.pallas_call(
        dispatch_kernel,
        out_shape=[shape((slots, heads, hdim), BF16), shape((4 * length + TAIL, hdim), BF16)],
        in_specs=[HBM] * 6,
        out_specs=[VMEM] * 2,
        scratch_shapes=[
            ints(rows),
            ints(pools),
            ints(pools),
            pltpu.VMEM((rows, heads, hdim), BF16),
            pltpu.VMEM((2, 2 * length, hdim), BF16),
            pltpu.VMEM((2, 2 * length, hdim), F32),
            ints(pools),
            pltpu.SemaphoreType.DMA((6,)),
        ],
        compiler_params=params(60),
        cost_estimate=pl.CostEstimate(flops=0, bytes_accessed=3_000_000, transcendentals=0),
        name="dispatch",
    )(
        row_prefix,
        owner_map,
        prefix_lengths,
        queries,
        prefix_keys.reshape(-1, hdim),
        prefix_values.reshape(-1, hdim),
    )

    arrived = lax.all_to_all(
        outgoing.reshape(pools, CAP, heads, hdim), "pool", split_axis=0, concat_axis=0, tiled=True
    ).reshape(slots, heads, hdim)
    asked = meet(arrived, "y", 1)

    pair, arrived_later = lax.optimization_barrier((meet(own, "y", 3), arrived))
    blocks = {(0, 0): own, (1, 0): pair}

    def attend(q, sources, earlier=None, times=1):
        span = len(sources) * length
        merging = earlier is not None
        return pl.pallas_call(
            functools.partial(attend_kernel, merging),
            out_shape=shape((slots + 3, heads, hdim), BF16),
            in_specs=[VMEM] * (1 + merging + len(sources)),
            out_specs=VMEM,
            compiler_params=params(30),
            cost_estimate=pl.CostEstimate(
                flops=6 * times * slots * heads * span * hdim,
                bytes_accessed=3_000_000,
                transcendentals=slots * heads * span,
            ),
            name="attend",
        )(q, *([earlier] if merging else []), *(blocks[source] for source in sources))

    first = attend(arrived_later, [(0, 0)])
    mine, pair, first = lax.optimization_barrier((own, pair, first))
    blocks.update({(0, 1): meet(mine, "core", 1), (1, 1): meet(pair, "core", 1)})
    direct, swapped = ((0, 0), (1, 0)), ((0, 1), (1, 1))
    answer = meet(attend(asked, swapped, attend(asked, direct, times=10)), "y", 1)
    own_part = attend(arrived_later, direct[1:] + swapped, first)
    merged = pl.pallas_call(
        merge_kernel,
        out_shape=shape((pools * (CAP * heads + GROUP), hdim), BF16),
        in_specs=[VMEM] * 2,
        out_specs=VMEM,
        compiler_params=params(8),
        cost_estimate=pl.CostEstimate(flops=0, bytes_accessed=1_000_000, transcendentals=0),
        name="merge",
    )(own_part, answer)
    merged, queries_later = lax.optimization_barrier((merged, queries))
    returned = lax.all_to_all(
        merged.reshape(pools, CAP * heads + GROUP, hdim),
        "pool",
        split_axis=0,
        concat_axis=0,
        tiled=True,
    ).reshape(-1, hdim)

    suffix = pl.pallas_call(
        suffix_kernel,
        out_shape=shape((rows, 2 * heads, hdim), F32),
        in_specs=[HBM, VMEM, VMEM, VMEM],
        out_specs=VMEM,
        scratch_shapes=[ints(rows), pltpu.SemaphoreType.DMA((1,))],
        compiler_params=params(8),
        cost_estimate=pl.CostEstimate(
            flops=4 * rows * heads * 128 * 128, bytes_accessed=2_000_000, transcendentals=0
        ),
        name="suffix",
    )(
        suffix_lengths,
        queries_later,
        suffix_keys.reshape(rows, -1, hdim),
        suffix_values.reshape(rows, -1, hdim),
    )

    attended = pl.pallas_call(
        combine_kernel,
        out_shape=shape((ring, rows, heads * hdim), BF16),
        in_specs=[HBM, HBM, VMEM, HBM],
        out_specs=VMEM,
        scratch_shapes=[
            ints(rows),
            ints(pools),
            pltpu.VMEM((rows, 2 * heads, hdim), F32),
            pltpu.VMEM((pools * (CAP * heads + GROUP), hdim), F32),
            pltpu.VMEM((rows * heads, hdim), F32),
            ints(pools),
            pltpu.SemaphoreType.DMA((3,)),
        ],
        compiler_params=params(8),
        cost_estimate=pl.CostEstimate(flops=0, bytes_accessed=1_000_000, transcendentals=0),
        name="combine",
    )(row_prefix, owner_map, returned, suffix)
    gathered = lax.all_to_all(attended, "y", split_axis=0, concat_axis=0, tiled=True)
    terms = pl.pallas_call(
        project_kernel,
        out_shape=shape((ring, 2, rows, columns), BF16),
        in_specs=[VMEM] * 3,
        out_specs=VMEM,
        compiler_params=params(16),
        cost_estimate=pl.CostEstimate(
            flops=4 * ring * rows * heads * hdim * columns,
            bytes_accessed=4_000_000,
            transcendentals=0,
        ),
        name="project",
    )(gathered, meet(gathered, "core", 1), out_weight)
    shared = lax.all_to_all(
        terms.reshape(lax.axis_size("head"), -1, columns),
        "head",
        split_axis=0,
        concat_axis=0,
        tiled=True,
    )
    return jnp.sum(shared.astype(F32), axis=0).astype(BF16)


def solution(mesh):
    pools, across, groups = mesh.devices.shape
    fine = Mesh(
        mesh.devices.reshape(pools, across // 2, 2, groups), ("pool", "y", "core", "head")
    )
    row = ("y", "core")
    every = ("pool", "y", "core")
    return jax.shard_map(
        body,
        mesh=fine,
        in_specs=(
            P(every, "head", None),
            P("pool", row, "head", None),
            P("pool", row, "head", None),
            P(every, None, "head", None),
            P(every, None, "head", None),
            P(every, None),
            P(),
            P(),
            P(every),
            P("head", row),
        ),
        out_specs=P(("pool", "head"), row),
        check_vma=False,
    )
```

```python
import functools
import math

import jax
import jax.numpy as jnp
from jax import lax
from jax.experimental import pallas as pl
from jax.experimental.pallas import tpu as pltpu
from jax.sharding import Mesh, PartitionSpec as P

LOWEST = -1e30
CAP = 3
GROUP = 8
HD = 128
SCALE = HD**-0.5
LOG2E = math.log2(math.e)
F32 = jnp.float32
BF16 = jnp.bfloat16

VMEM = pl.BlockSpec(memory_space=pltpu.VMEM)
HBM = pl.BlockSpec(memory_space=pltpu.HBM)
TAIL = 16


def params(mib):
    return pltpu.CompilerParams(vmem_limit_bytes=mib * 1024 * 1024)


def split3(value):
    high = value.astype(BF16).astype(F32)
    rest = value - high
    middle = rest.astype(BF16).astype(F32)
    return high, middle, (rest - middle).astype(BF16).astype(F32)


def slot_of(row, row_prefix_ref, owner_ref, count_ref):
    owner = owner_ref[row_prefix_ref[row]]
    place = count_ref[owner]
    count_ref[owner] = place + 1
    return owner, place


def fetch(pairs, sems):
    copies = [pltpu.make_async_copy(*pair, sems.at[i]) for i, pair in enumerate(pairs)]
    for copy in copies:
        copy.start()
    return copies


def dispatch_kernel(
    row_prefix_hbm, owner_hbm, lengths_hbm, q_hbm, k_hbm, v_hbm, out_ref, block_ref,
    row_prefix_ref, owner_ref, lengths_ref, q_ref, mixed, held, count_ref, sems,
):
    copies = fetch(
        (
            (row_prefix_hbm, row_prefix_ref),
            (owner_hbm, owner_ref),
            (lengths_hbm, lengths_ref),
            (q_hbm, q_ref),
            (k_hbm, mixed.at[0]),
            (v_hbm, mixed.at[1]),
        ),
        sems,
    )
    pools = owner_ref.shape[0]
    length = mixed.shape[1] // 2
    for p in range(pools):
        count_ref[p] = 0
    out_ref[...] = jnp.zeros_like(out_ref)
    for copy in copies[:4]:
        copy.wait()
    for r in range(q_ref.shape[0]):
        owner, place = slot_of(r, row_prefix_ref, owner_ref, count_ref)
        out_ref[owner * CAP + place] = q_ref[r]
    pool = lax.axis_index("pool")
    seen = -(lax.axis_index("y") * 2 + lax.axis_index("core")) * length
    for p in range(pools):
        seen += jnp.where(owner_ref[p] == pool, lengths_ref[p], 0)
    tail = (TAIL, HD)
    token = lax.broadcasted_iota(jnp.int32, tail, 0) * HD + lax.broadcasted_iota(jnp.int32, tail, 1)
    block_ref[pl.ds(4 * length, TAIL), :] = jnp.where(token < seen, 0.0, LOWEST).astype(BF16)
    for n in range(2):
        copies[4 + n].wait()
        held[n] = mixed[n].astype(F32)
        for g in range(2):
            block_ref[pl.ds((2 * n + g) * length, length), :] = held[
                n, pl.ds(g, length, stride=2), :
            ].astype(BF16)


def unpack_lse(ref):
    slots = ref.shape[0] - 3
    high, middle, low = (ref[slots + i].astype(F32) for i in range(3))
    return (low + middle) + high


def attend_kernel(merging, q_ref, *refs):
    earlier_ref = refs[0] if merging else None
    blocks, out_ref = refs[int(merging) : -1], refs[-1]
    slots = q_ref.shape[0]
    step_slots = math.gcd(24, slots)
    length = (blocks[0].shape[0] - TAIL) // 4
    width = min(512, length)
    units = [(start, g) for start in range(0, slots, step_slots) for g in range(2)]
    pieces = [(block, at) for block in blocks for at in range(0, length, width)]
    lane = lax.broadcasted_iota(jnp.int32, (GROUP, 128), 1)
    ones = jnp.ones((width, HD), BF16)
    tails = [block[pl.ds(4 * length, TAIL), :].astype(F32) for block in blocks]
    biases = [
        jnp.concatenate(
            [tail[row : row + 1] for row in range(at // HD, (at + width) // HD)], axis=1
        )
        for tail in tails
        for at in range(0, length, width)
    ]

    def query(unit):
        start, g = unit
        held = q_ref[pl.ds(start, step_slots)].astype(F32)[:, g * GROUP : (g + 1) * GROUP, :]
        return held.reshape(step_slots * GROUP, HD).astype(BF16)

    def score(q, g, n):
        block, at = pieces[n]
        keys = block[pl.ds(g * length + at, width), :]
        return (
            lax.dot_general(q, keys, (((1,), (1,)), ((), ())), preferred_element_type=F32)
            + biases[n]
        )

    if merging:
        earlier_lse = unpack_lse(earlier_ref)
    packed = [jnp.zeros((GROUP, 128), F32)] * 2
    kept = {}
    q = query(units[0])
    scores = [score(q, units[0][1], n) for n in range(len(pieces))]
    for i, (start, g) in enumerate(units):
        peak = functools.reduce(
            jnp.maximum, [jnp.max(part, axis=1, keepdims=True) for part in scores]
        )
        peak = jnp.maximum(peak, 0.1 * LOWEST)
        coming = []
        both = None
        if i + 1 < len(units):
            q = query(units[i + 1])
        for n, (block, at) in enumerate(pieces):
            weights = jnp.exp2((scores[n] - peak) * (SCALE * LOG2E)).astype(BF16)
            if i + 1 < len(units):
                coming.append(score(q, units[i + 1][1], n))
            values = jnp.concatenate(
                [block[pl.ds((2 + g) * length + at, width), :], ones], axis=1
            )
            term = jnp.dot(weights, values, preferred_element_type=F32)
            both = term if both is None else both + term
        scores = coming
        total = both[:, HD:]
        live = total > 0
        safe = jnp.where(live, total, 1.0)
        kept[g] = (both[:, :HD] / safe).reshape(step_slots, GROUP, HD)
        lse = jnp.where(live, peak * SCALE + jnp.log(safe), LOWEST)
        lse = lse.reshape(step_slots, GROUP, HD)
        if merging:
            half = slice(g * GROUP, (g + 1) * GROUP)
            before = jnp.stack(
                [
                    jnp.broadcast_to(earlier_lse[half, s : s + 1], (GROUP, HD))
                    for s in range(start, start + step_slots)
                ]
            )
            result = earlier_ref[pl.ds(start, step_slots)].astype(F32)[:, half, :]
            top = jnp.maximum(lse, before)
            a = jnp.exp(lse - top)
            b = jnp.exp(before - top)
            kept[g] = (a * kept[g] + b * result) / (a + b)
            lse = top + jnp.log(a + b)
        for s in range(step_slots):
            packed[g] = jnp.where(lane == start + s, lse[s], packed[g])
        if g == 1:
            out_ref[pl.ds(start, step_slots)] = jnp.concatenate(
                [kept[0], kept[1]], axis=1
            ).astype(BF16)
    for i, plane in enumerate(split3(jnp.concatenate(packed, axis=0))):
        out_ref[slots + i] = plane.astype(BF16)


def merge_kernel(a_ref, b_ref, out_ref):
    blocks = (a_ref, b_ref)
    slots = a_ref.shape[0] - 3
    pools = slots // CAP
    lses = [unpack_lse(ref) for ref in blocks]
    top = functools.reduce(jnp.maximum, lses)
    shares = [jnp.exp(lse - top) for lse in lses]
    total = functools.reduce(jnp.add, shares)
    weights = [share / total for share in shares]
    planes = split3(top + jnp.log(total))
    lane = lax.broadcasted_iota(jnp.int32, (GROUP, 128), 1)
    for pair in range(0, pools, 2):
        rows = []
        for p in (pair, pair + 1):
            for s in range(p * CAP, (p + 1) * CAP):
                terms = [
                    weight[:, s : s + 1] * ref[s].astype(F32) for weight, ref in zip(weights, blocks)
                ]
                rows.append(functools.reduce(jnp.add, terms))
            tile = jnp.zeros((GROUP, 128), F32)
            for i, plane in enumerate(planes):
                for g in range(2):
                    at = i * 16 + g * 8
                    moved = plane[g * GROUP : (g + 1) * GROUP]
                    shift = (at - p * CAP) % 128
                    if shift:
                        moved = pltpu.roll(moved, shift, 1)
                    tile = jnp.where((lane >= at) & (lane < at + CAP), moved, tile)
            rows.append(tile)
        height = CAP * 16 + GROUP
        out_ref[pl.ds(pair * height, 2 * height), :] = jnp.concatenate(rows, axis=0).astype(BF16)


def suffix_kernel(length_hbm, q_ref, k_ref, v_ref, out_ref, length_ref, sems):
    fetch(((length_hbm, length_ref),), sems)[0].wait()
    span = k_ref.shape[1]
    column = lax.broadcasted_iota(jnp.int32, (2 * GROUP, span), 1)
    head = lax.broadcasted_iota(jnp.int32, (2 * GROUP, span), 0)
    same = (column & 1) == head // GROUP
    for r in range(q_ref.shape[0]):
        scores = lax.dot_general(
            q_ref[r], k_ref[r], (((1,), (1,)), ((), ())), preferred_element_type=F32
        )
        visible = same & (column < 2 * length_ref[r])
        scores = jnp.where(visible, scores * SCALE, LOWEST)
        peak = jnp.max(scores, axis=1, keepdims=True)
        powers = jnp.exp(scores - peak)
        total = jnp.sum(powers, axis=1, keepdims=True)
        summed = jnp.dot(powers.astype(BF16), v_ref[r], preferred_element_type=F32)
        out_ref[r, : 2 * GROUP] = summed / total
        out_ref[r, 2 * GROUP :] = jnp.broadcast_to(peak + jnp.log(total), (2 * GROUP, HD))


def combine_kernel(
    row_prefix_hbm, owner_hbm, got_ref, suffix_hbm, out_ref,
    row_prefix_ref, owner_ref, suffix_ref, wide, mixed, count_ref, sems,
):
    copies = fetch(
        (
            (row_prefix_hbm, row_prefix_ref),
            (owner_hbm, owner_ref),
            (suffix_hbm, suffix_ref),
        ),
        sems,
    )
    rows = suffix_ref.shape[0]
    height = CAP * 16 + GROUP
    for p in range(owner_ref.shape[0]):
        count_ref[p] = 0
    wide[...] = got_ref[...].astype(F32)
    for copy in copies:
        copy.wait()
    lane = lax.broadcasted_iota(jnp.int32, (GROUP, 128), 1)
    for r in range(rows):
        owner, place = slot_of(r, row_prefix_ref, owner_ref, count_ref)
        base = owner * height
        prefix = wide[pl.ds(pl.multiple_of(base + place * 16, 8), 16), :]
        tile = wide[pl.ds(pl.multiple_of(base + CAP * 16, 8), GROUP), :]
        lses = []
        for g in range(2):
            chosen = ((lane & 15) == place + g * 8) & (lane < 48)
            lses.append(jnp.sum(jnp.where(chosen, tile, 0.0), axis=1, keepdims=True))
        prefix_lse = jnp.broadcast_to(jnp.concatenate(lses, axis=0), (2 * GROUP, HD))
        suffix_lse = suffix_ref[r, 2 * GROUP :]
        highest = jnp.maximum(prefix_lse, suffix_lse)
        a = jnp.exp(prefix_lse - highest)
        b = jnp.exp(suffix_lse - highest)
        mixed[r * 16 : (r + 1) * 16, :] = (a * prefix + b * suffix_ref[r, : 2 * GROUP]) / (a + b)
    for h in range(2 * GROUP):
        piece = mixed[pl.ds(h, rows, stride=16), :].astype(BF16)
        for n in range(out_ref.shape[0]):
            out_ref[n, :, h * HD : (h + 1) * HD] = piece


def project_kernel(own_ref, other_ref, w_ref, out_ref):
    count, rows, depth = own_ref.shape
    core = lax.axis_index("core")
    both = jnp.concatenate(
        [own_ref[...].reshape(count * rows, depth), other_ref[...].reshape(count * rows, depth)],
        axis=0,
    )
    terms = jnp.dot(both, w_ref[...], preferred_element_type=F32).astype(BF16)
    terms = terms.reshape(2, count, rows, -1)
    for n in range(count):
        out_ref[n, core] = terms[0, n]
        out_ref[n, 1 - core] = terms[1, n]


def body(
    queries,
    prefix_keys,
    prefix_values,
    suffix_keys,
    suffix_values,
    row_prefix,
    owner_map,
    prefix_lengths,
    suffix_lengths,
    out_weight,
):
    rows, heads, hdim = queries.shape
    row_prefix = row_prefix.reshape(-1)
    pools = lax.axis_size("pool")
    ring = lax.axis_size("y")
    slots = pools * CAP
    columns = out_weight.shape[1]
    shape = jax.ShapeDtypeStruct

    def meet(value, axis, apart):
        pairs = [(i, i ^ apart) for i in range(lax.axis_size(axis))]
        return lax.ppermute(value, axis, pairs)

    def ints(count):
        return pltpu.SMEM((count,), jnp.int32)

    length = prefix_keys.shape[1]
    outgoing, own = pl.pallas_call(
        dispatch_kernel,
        out_shape=[shape((slots, heads, hdim), BF16), shape((4 * length + TAIL, hdim), BF16)],
        in_specs=[HBM] * 6,
        out_specs=[VMEM] * 2,
        scratch_shapes=[
            ints(rows),
            ints(pools),
            ints(pools),
            pltpu.VMEM((rows, heads, hdim), BF16),
            pltpu.VMEM((2, 2 * length, hdim), BF16),
            pltpu.VMEM((2, 2 * length, hdim), F32),
            ints(pools),
            pltpu.SemaphoreType.DMA((6,)),
        ],
        compiler_params=params(60),
        cost_estimate=pl.CostEstimate(flops=0, bytes_accessed=3_000_000, transcendentals=0),
        name="dispatch",
    )(
        row_prefix,
        owner_map,
        prefix_lengths,
        queries,
        prefix_keys.reshape(-1, hdim),
        prefix_values.reshape(-1, hdim),
    )

    arrived = lax.all_to_all(
        outgoing.reshape(pools, CAP, heads, hdim), "pool", split_axis=0, concat_axis=0, tiled=True
    ).reshape(slots, heads, hdim)
    asked = meet(arrived, "y", 1)

    pair, arrived_later = lax.optimization_barrier((meet(own, "y", 3), arrived))
    blocks = {(0, 0): own, (1, 0): pair}

    def attend(q, sources, earlier=None, times=1):
        span = len(sources) * length
        merging = earlier is not None
        return pl.pallas_call(
            functools.partial(attend_kernel, merging),
            out_shape=shape((slots + 3, heads, hdim), BF16),
            in_specs=[VMEM] * (1 + merging + len(sources)),
            out_specs=VMEM,
            compiler_params=params(30),
            cost_estimate=pl.CostEstimate(
                flops=6 * times * slots * heads * span * hdim,
                bytes_accessed=3_000_000,
                transcendentals=slots * heads * span,
            ),
            name="attend",
        )(q, *([earlier] if merging else []), *(blocks[source] for source in sources))

    blocks.update({(0, 1): meet(own, "core", 1), (1, 1): meet(pair, "core", 1)})
    others = ((0, 0), (0, 1), (1, 1))
    answer = meet(attend(asked, others, attend(asked, [(1, 0)], times=20)), "y", 1)
    own_part = attend(arrived_later, ((1, 0),) + others)
    merged = pl.pallas_call(
        merge_kernel,
        out_shape=shape((pools * (CAP * heads + GROUP), hdim), BF16),
        in_specs=[VMEM] * 2,
        out_specs=VMEM,
        compiler_params=params(8),
        cost_estimate=pl.CostEstimate(flops=0, bytes_accessed=1_000_000, transcendentals=0),
        name="merge",
    )(own_part, answer)
    merged, queries_later = lax.optimization_barrier((merged, queries))
    returned = lax.all_to_all(
        merged.reshape(pools, CAP * heads + GROUP, hdim),
        "pool",
        split_axis=0,
        concat_axis=0,
        tiled=True,
    ).reshape(-1, hdim)

    suffix = pl.pallas_call(
        suffix_kernel,
        out_shape=shape((rows, 2 * heads, hdim), F32),
        in_specs=[HBM, VMEM, VMEM, VMEM],
        out_specs=VMEM,
        scratch_shapes=[ints(rows), pltpu.SemaphoreType.DMA((1,))],
        compiler_params=params(8),
        cost_estimate=pl.CostEstimate(
            flops=4 * rows * heads * 128 * 128, bytes_accessed=2_000_000, transcendentals=0
        ),
        name="suffix",
    )(
        suffix_lengths,
        queries_later,
        suffix_keys.reshape(rows, -1, hdim),
        suffix_values.reshape(rows, -1, hdim),
    )

    attended = pl.pallas_call(
        combine_kernel,
        out_shape=shape((ring, rows, heads * hdim), BF16),
        in_specs=[HBM, HBM, VMEM, HBM],
        out_specs=VMEM,
        scratch_shapes=[
            ints(rows),
            ints(pools),
            pltpu.VMEM((rows, 2 * heads, hdim), F32),
            pltpu.VMEM((pools * (CAP * heads + GROUP), hdim), F32),
            pltpu.VMEM((rows * heads, hdim), F32),
            ints(pools),
            pltpu.SemaphoreType.DMA((3,)),
        ],
        compiler_params=params(8),
        cost_estimate=pl.CostEstimate(flops=0, bytes_accessed=1_000_000, transcendentals=0),
        name="combine",
    )(row_prefix, owner_map, returned, suffix)
    gathered = lax.all_to_all(attended, "y", split_axis=0, concat_axis=0, tiled=True)
    terms = pl.pallas_call(
        project_kernel,
        out_shape=shape((ring, 2, rows, columns), BF16),
        in_specs=[VMEM] * 3,
        out_specs=VMEM,
        compiler_params=params(16),
        cost_estimate=pl.CostEstimate(
            flops=4 * ring * rows * heads * hdim * columns,
            bytes_accessed=4_000_000,
            transcendentals=0,
        ),
        name="project",
    )(gathered, meet(gathered, "core", 1), out_weight)
    shared = lax.all_to_all(
        terms.reshape(lax.axis_size("head"), -1, columns),
        "head",
        split_axis=0,
        concat_axis=0,
        tiled=True,
    )
    return jnp.sum(shared.astype(F32), axis=0).astype(BF16)


def solution(mesh):
    pools, across, groups = mesh.devices.shape
    fine = Mesh(
        mesh.devices.reshape(pools, across // 2, 2, groups), ("pool", "y", "core", "head")
    )
    row = ("y", "core")
    every = ("pool", "y", "core")
    return jax.shard_map(
        body,
        mesh=fine,
        in_specs=(
            P(every, "head", None),
            P("pool", row, "head", None),
            P("pool", row, "head", None),
            P(every, None, "head", None),
            P(every, None, "head", None),
            P(every, None),
            P(),
            P(),
            P(every),
            P("head", row),
        ),
        out_specs=P(("pool", "head"), row),
        check_vma=False,
    )
```

```python
import functools
import math

import jax
import jax.numpy as jnp
from jax import lax
from jax.experimental import pallas as pl
from jax.experimental.pallas import tpu as pltpu
from jax.sharding import Mesh, PartitionSpec as P

LOWEST = -1e30
CAP = 3
GROUP = 8
HD = 128
SCALE = HD**-0.5
LOG2E = math.log2(math.e)
F32 = jnp.float32
BF16 = jnp.bfloat16

VMEM = pl.BlockSpec(memory_space=pltpu.VMEM)
HBM = pl.BlockSpec(memory_space=pltpu.HBM)
TAIL = 16


def params(mib):
    return pltpu.CompilerParams(vmem_limit_bytes=mib * 1024 * 1024)


def split3(value):
    high = value.astype(BF16).astype(F32)
    rest = value - high
    middle = rest.astype(BF16).astype(F32)
    return high, middle, (rest - middle).astype(BF16).astype(F32)


def slot_of(row, row_prefix_ref, owner_ref, count_ref):
    owner = owner_ref[row_prefix_ref[row]]
    place = count_ref[owner]
    count_ref[owner] = place + 1
    return owner, place


def fetch(pairs, sems):
    copies = [pltpu.make_async_copy(*pair, sems.at[i]) for i, pair in enumerate(pairs)]
    for copy in copies:
        copy.start()
    return copies


def dispatch_kernel(
    row_prefix_hbm, owner_hbm, lengths_hbm, q_hbm, k_hbm, v_hbm, out_ref, block_ref,
    row_prefix_ref, owner_ref, lengths_ref, q_ref, mixed, held, count_ref, sems,
):
    copies = fetch(
        (
            (row_prefix_hbm, row_prefix_ref),
            (owner_hbm, owner_ref),
            (lengths_hbm, lengths_ref),
            (q_hbm, q_ref),
            (k_hbm, mixed.at[0]),
            (v_hbm, mixed.at[1]),
        ),
        sems,
    )
    pools = owner_ref.shape[0]
    length = mixed.shape[1] // 2
    for p in range(pools):
        count_ref[p] = 0
    out_ref[...] = jnp.zeros_like(out_ref)
    for copy in copies[:4]:
        copy.wait()
    for r in range(q_ref.shape[0]):
        owner, place = slot_of(r, row_prefix_ref, owner_ref, count_ref)
        out_ref[owner * CAP + place] = q_ref[r]
    pool = lax.axis_index("pool")
    seen = -(lax.axis_index("y") * 2 + lax.axis_index("core")) * length
    for p in range(pools):
        seen += jnp.where(owner_ref[p] == pool, lengths_ref[p], 0)
    tail = (TAIL, HD)
    token = lax.broadcasted_iota(jnp.int32, tail, 0) * HD + lax.broadcasted_iota(jnp.int32, tail, 1)
    block_ref[pl.ds(4 * length, TAIL), :] = jnp.where(token < seen, 0.0, LOWEST).astype(BF16)
    for n in range(2):
        copies[4 + n].wait()
        held[n] = mixed[n].astype(F32)
        for g in range(2):
            block_ref[pl.ds((2 * n + g) * length, length), :] = held[
                n, pl.ds(g, length, stride=2), :
            ].astype(BF16)


def unpack_lse(ref):
    slots = ref.shape[0] - 3
    high, middle, low = (ref[slots + i].astype(F32) for i in range(3))
    return (low + middle) + high


def attend_kernel(merging, q_ref, *refs):
    earlier_ref = refs[0] if merging else None
    blocks, out_ref = refs[int(merging) : -1], refs[-1]
    slots = q_ref.shape[0]
    step_slots = math.gcd(48, slots)
    length = (blocks[0].shape[0] - TAIL) // 4
    width = min(512, length)
    units = [(start, g) for start in range(0, slots, step_slots) for g in range(2)]
    pieces = [(block, at) for block in blocks for at in range(0, length, width)]
    lane = lax.broadcasted_iota(jnp.int32, (GROUP, 128), 1)
    ones = jnp.ones((width, HD), BF16)
    tails = [block[pl.ds(4 * length, TAIL), :].astype(F32) for block in blocks]
    biases = [
        jnp.concatenate(
            [tail[row : row + 1] for row in range(at // HD, (at + width) // HD)], axis=1
        )
        for tail in tails
        for at in range(0, length, width)
    ]

    def query(unit):
        start, g = unit
        held = q_ref[pl.ds(start, step_slots)].astype(F32)[:, g * GROUP : (g + 1) * GROUP, :]
        return held.reshape(step_slots * GROUP, HD).astype(BF16)

    def score(q, g, n):
        block, at = pieces[n]
        keys = block[pl.ds(g * length + at, width), :]
        return (
            lax.dot_general(q, keys, (((1,), (1,)), ((), ())), preferred_element_type=F32)
            + biases[n]
        )

    if merging:
        earlier_lse = unpack_lse(earlier_ref)
    packed = [jnp.zeros((GROUP, 128), F32)] * 2
    kept = {}
    q = query(units[0])
    scores = [score(q, units[0][1], n) for n in range(len(pieces))]
    for i, (start, g) in enumerate(units):
        peak = functools.reduce(
            jnp.maximum, [jnp.max(part, axis=1, keepdims=True) for part in scores]
        )
        peak = jnp.maximum(peak, 0.1 * LOWEST)
        coming = []
        both = None
        if i + 1 < len(units):
            q = query(units[i + 1])
        for n, (block, at) in enumerate(pieces):
            weights = jnp.exp2((scores[n] - peak) * (SCALE * LOG2E)).astype(BF16)
            if i + 1 < len(units):
                coming.append(score(q, units[i + 1][1], n))
            values = jnp.concatenate(
                [block[pl.ds((2 + g) * length + at, width), :], ones], axis=1
            )
            term = jnp.dot(weights, values, preferred_element_type=F32)
            both = term if both is None else both + term
        scores = coming
        total = both[:, HD:]
        live = total > 0
        safe = jnp.where(live, total, 1.0)
        kept[g] = (both[:, :HD] / safe).reshape(step_slots, GROUP, HD)
        lse = jnp.where(live, peak * SCALE + jnp.log(safe), LOWEST)
        lse = lse.reshape(step_slots, GROUP, HD)
        if merging:
            half = slice(g * GROUP, (g + 1) * GROUP)
            before = jnp.stack(
                [
                    jnp.broadcast_to(earlier_lse[half, s : s + 1], (GROUP, HD))
                    for s in range(start, start + step_slots)
                ]
            )
            result = earlier_ref[pl.ds(start, step_slots)].astype(F32)[:, half, :]
            top = jnp.maximum(lse, before)
            a = jnp.exp(lse - top)
            b = jnp.exp(before - top)
            kept[g] = (a * kept[g] + b * result) / (a + b)
            lse = top + jnp.log(a + b)
        for s in range(step_slots):
            packed[g] = jnp.where(lane == start + s, lse[s], packed[g])
        if g == 1:
            out_ref[pl.ds(start, step_slots)] = jnp.concatenate(
                [kept[0], kept[1]], axis=1
            ).astype(BF16)
    for i, plane in enumerate(split3(jnp.concatenate(packed, axis=0))):
        out_ref[slots + i] = plane.astype(BF16)


def merge_kernel(a_ref, b_ref, out_ref):
    blocks = (a_ref, b_ref)
    slots = a_ref.shape[0] - 3
    pools = slots // CAP
    lses = [unpack_lse(ref) for ref in blocks]
    top = functools.reduce(jnp.maximum, lses)
    shares = [jnp.exp(lse - top) for lse in lses]
    total = functools.reduce(jnp.add, shares)
    weights = [share / total for share in shares]
    planes = split3(top + jnp.log(total))
    lane = lax.broadcasted_iota(jnp.int32, (GROUP, 128), 1)
    for pair in range(0, pools, 2):
        rows = []
        for p in (pair, pair + 1):
            for s in range(p * CAP, (p + 1) * CAP):
                terms = [
                    weight[:, s : s + 1] * ref[s].astype(F32) for weight, ref in zip(weights, blocks)
                ]
                rows.append(functools.reduce(jnp.add, terms))
            tile = jnp.zeros((GROUP, 128), F32)
            for i, plane in enumerate(planes):
                for g in range(2):
                    at = i * 16 + g * 8
                    moved = plane[g * GROUP : (g + 1) * GROUP]
                    shift = (at - p * CAP) % 128
                    if shift:
                        moved = pltpu.roll(moved, shift, 1)
                    tile = jnp.where((lane >= at) & (lane < at + CAP), moved, tile)
            rows.append(tile)
        height = CAP * 16 + GROUP
        out_ref[pl.ds(pair * height, 2 * height), :] = jnp.concatenate(rows, axis=0).astype(BF16)


def suffix_kernel(length_hbm, q_ref, k_ref, v_ref, out_ref, length_ref, sems):
    fetch(((length_hbm, length_ref),), sems)[0].wait()
    span = k_ref.shape[1]
    column = lax.broadcasted_iota(jnp.int32, (2 * GROUP, span), 1)
    head = lax.broadcasted_iota(jnp.int32, (2 * GROUP, span), 0)
    same = (column & 1) == head // GROUP
    for r in range(q_ref.shape[0]):
        scores = lax.dot_general(
            q_ref[r], k_ref[r], (((1,), (1,)), ((), ())), preferred_element_type=F32
        )
        visible = same & (column < 2 * length_ref[r])
        scores = jnp.where(visible, scores * SCALE, LOWEST)
        peak = jnp.max(scores, axis=1, keepdims=True)
        powers = jnp.exp(scores - peak)
        total = jnp.sum(powers, axis=1, keepdims=True)
        summed = jnp.dot(powers.astype(BF16), v_ref[r], preferred_element_type=F32)
        out_ref[r, : 2 * GROUP] = summed / total
        out_ref[r, 2 * GROUP :] = jnp.broadcast_to(peak + jnp.log(total), (2 * GROUP, HD))


def combine_kernel(
    row_prefix_hbm, owner_hbm, got_ref, suffix_hbm, out_ref,
    row_prefix_ref, owner_ref, suffix_ref, wide, mixed, count_ref, sems,
):
    copies = fetch(
        (
            (row_prefix_hbm, row_prefix_ref),
            (owner_hbm, owner_ref),
            (suffix_hbm, suffix_ref),
        ),
        sems,
    )
    rows = suffix_ref.shape[0]
    height = CAP * 16 + GROUP
    for p in range(owner_ref.shape[0]):
        count_ref[p] = 0
    wide[...] = got_ref[...].astype(F32)
    for copy in copies:
        copy.wait()
    lane = lax.broadcasted_iota(jnp.int32, (GROUP, 128), 1)
    for r in range(rows):
        owner, place = slot_of(r, row_prefix_ref, owner_ref, count_ref)
        base = owner * height
        prefix = wide[pl.ds(pl.multiple_of(base + place * 16, 8), 16), :]
        tile = wide[pl.ds(pl.multiple_of(base + CAP * 16, 8), GROUP), :]
        lses = []
        for g in range(2):
            chosen = ((lane & 15) == place + g * 8) & (lane < 48)
            lses.append(jnp.sum(jnp.where(chosen, tile, 0.0), axis=1, keepdims=True))
        prefix_lse = jnp.broadcast_to(jnp.concatenate(lses, axis=0), (2 * GROUP, HD))
        suffix_lse = suffix_ref[r, 2 * GROUP :]
        highest = jnp.maximum(prefix_lse, suffix_lse)
        a = jnp.exp(prefix_lse - highest)
        b = jnp.exp(suffix_lse - highest)
        mixed[r * 16 : (r + 1) * 16, :] = (a * prefix + b * suffix_ref[r, : 2 * GROUP]) / (a + b)
    for h in range(2 * GROUP):
        piece = mixed[pl.ds(h, rows, stride=16), :].astype(BF16)
        for n in range(out_ref.shape[0]):
            out_ref[n, :, h * HD : (h + 1) * HD] = piece


def project_kernel(own_ref, other_ref, w_ref, out_ref):
    count, rows, depth = own_ref.shape
    core = lax.axis_index("core")
    both = jnp.concatenate(
        [own_ref[...].reshape(count * rows, depth), other_ref[...].reshape(count * rows, depth)],
        axis=0,
    )
    terms = jnp.dot(both, w_ref[...], preferred_element_type=F32).astype(BF16)
    terms = terms.reshape(2, count, rows, -1)
    for n in range(count):
        out_ref[n, core] = terms[0, n]
        out_ref[n, 1 - core] = terms[1, n]


def body(
    queries,
    prefix_keys,
    prefix_values,
    suffix_keys,
    suffix_values,
    row_prefix,
    owner_map,
    prefix_lengths,
    suffix_lengths,
    out_weight,
):
    rows, heads, hdim = queries.shape
    row_prefix = row_prefix.reshape(-1)
    pools = lax.axis_size("pool")
    ring = lax.axis_size("y")
    slots = pools * CAP
    columns = out_weight.shape[1]
    shape = jax.ShapeDtypeStruct

    def meet(value, axis, apart):
        pairs = [(i, i ^ apart) for i in range(lax.axis_size(axis))]
        return lax.ppermute(value, axis, pairs)

    def ints(count):
        return pltpu.SMEM((count,), jnp.int32)

    length = prefix_keys.shape[1]
    outgoing, own = pl.pallas_call(
        dispatch_kernel,
        out_shape=[shape((slots, heads, hdim), BF16), shape((4 * length + TAIL, hdim), BF16)],
        in_specs=[HBM] * 6,
        out_specs=[VMEM] * 2,
        scratch_shapes=[
            ints(rows),
            ints(pools),
            ints(pools),
            pltpu.VMEM((rows, heads, hdim), BF16),
            pltpu.VMEM((2, 2 * length, hdim), BF16),
            pltpu.VMEM((2, 2 * length, hdim), F32),
            ints(pools),
            pltpu.SemaphoreType.DMA((6,)),
        ],
        compiler_params=params(60),
        cost_estimate=pl.CostEstimate(flops=0, bytes_accessed=3_000_000, transcendentals=0),
        name="dispatch",
    )(
        row_prefix,
        owner_map,
        prefix_lengths,
        queries,
        prefix_keys.reshape(-1, hdim),
        prefix_values.reshape(-1, hdim),
    )

    arrived = lax.all_to_all(
        outgoing.reshape(pools, CAP, heads, hdim), "pool", split_axis=0, concat_axis=0, tiled=True
    ).reshape(slots, heads, hdim)
    asked = meet(arrived, "y", 1)

    pair, arrived_later = lax.optimization_barrier((meet(own, "y", 3), arrived))
    blocks = {(0, 0): own, (1, 0): pair}

    def attend(q, sources, earlier=None, times=1):
        span = len(sources) * length
        merging = earlier is not None
        return pl.pallas_call(
            functools.partial(attend_kernel, merging),
            out_shape=shape((slots + 3, heads, hdim), BF16),
            in_specs=[VMEM] * (1 + merging + len(sources)),
            out_specs=VMEM,
            compiler_params=params(30),
            cost_estimate=pl.CostEstimate(
                flops=6 * times * slots * heads * span * hdim,
                bytes_accessed=3_000_000,
                transcendentals=slots * heads * span,
            ),
            name="attend",
        )(q, *([earlier] if merging else []), *(blocks[source] for source in sources))

    blocks.update({(0, 1): meet(own, "core", 1), (1, 1): meet(pair, "core", 1)})
    others = ((0, 0), (0, 1), (1, 1))
    answer = meet(attend(asked, others, attend(asked, [(1, 0)], times=20)), "y", 1)
    own_part = attend(arrived_later, ((1, 0),) + others)
    merged = pl.pallas_call(
        merge_kernel,
        out_shape=shape((pools * (CAP * heads + GROUP), hdim), BF16),
        in_specs=[VMEM] * 2,
        out_specs=VMEM,
        compiler_params=params(8),
        cost_estimate=pl.CostEstimate(flops=0, bytes_accessed=1_000_000, transcendentals=0),
        name="merge",
    )(own_part, answer)
    merged, queries_later = lax.optimization_barrier((merged, queries))
    returned = lax.all_to_all(
        merged.reshape(pools, CAP * heads + GROUP, hdim),
        "pool",
        split_axis=0,
        concat_axis=0,
        tiled=True,
    ).reshape(-1, hdim)

    suffix = pl.pallas_call(
        suffix_kernel,
        out_shape=shape((rows, 2 * heads, hdim), F32),
        in_specs=[HBM, VMEM, VMEM, VMEM],
        out_specs=VMEM,
        scratch_shapes=[ints(rows), pltpu.SemaphoreType.DMA((1,))],
        compiler_params=params(8),
        cost_estimate=pl.CostEstimate(
            flops=4 * rows * heads * 128 * 128, bytes_accessed=2_000_000, transcendentals=0
        ),
        name="suffix",
    )(
        suffix_lengths,
        queries_later,
        suffix_keys.reshape(rows, -1, hdim),
        suffix_values.reshape(rows, -1, hdim),
    )

    attended = pl.pallas_call(
        combine_kernel,
        out_shape=shape((ring, rows, heads * hdim), BF16),
        in_specs=[HBM, HBM, VMEM, HBM],
        out_specs=VMEM,
        scratch_shapes=[
            ints(rows),
            ints(pools),
            pltpu.VMEM((rows, 2 * heads, hdim), F32),
            pltpu.VMEM((pools * (CAP * heads + GROUP), hdim), F32),
            pltpu.VMEM((rows * heads, hdim), F32),
            ints(pools),
            pltpu.SemaphoreType.DMA((3,)),
        ],
        compiler_params=params(8),
        cost_estimate=pl.CostEstimate(flops=0, bytes_accessed=1_000_000, transcendentals=0),
        name="combine",
    )(row_prefix, owner_map, returned, suffix)
    gathered = lax.all_to_all(attended, "y", split_axis=0, concat_axis=0, tiled=True)
    terms = pl.pallas_call(
        project_kernel,
        out_shape=shape((ring, 2, rows, columns), BF16),
        in_specs=[VMEM] * 3,
        out_specs=VMEM,
        compiler_params=params(16),
        cost_estimate=pl.CostEstimate(
            flops=4 * ring * rows * heads * hdim * columns,
            bytes_accessed=4_000_000,
            transcendentals=0,
        ),
        name="project",
    )(gathered, meet(gathered, "core", 1), out_weight)
    shared = lax.all_to_all(
        terms.reshape(lax.axis_size("head"), -1, columns),
        "head",
        split_axis=0,
        concat_axis=0,
        tiled=True,
    )
    return jnp.sum(shared.astype(F32), axis=0).astype(BF16)


def solution(mesh):
    pools, across, groups = mesh.devices.shape
    fine = Mesh(
        mesh.devices.reshape(pools, across // 2, 2, groups), ("pool", "y", "core", "head")
    )
    row = ("y", "core")
    every = ("pool", "y", "core")
    return jax.shard_map(
        body,
        mesh=fine,
        in_specs=(
            P(every, "head", None),
            P("pool", row, "head", None),
            P("pool", row, "head", None),
            P(every, None, "head", None),
            P(every, None, "head", None),
            P(every, None),
            P(),
            P(),
            P(every),
            P("head", row),
        ),
        out_specs=P(("pool", "head"), row),
        check_vma=False,
    )
```
